32 devices in a mesh: fsdp: 4 (over y, x), ctx: 4 (over z), tp: 2 (over core).
Axes of the slice: x: 2, y: 2, z: 4, core: 2. Of those that a mesh axis runs over, the one named last changes fastest.
Arguments:
- tokens: bfloat16 [32768, 768], P(('fsdp', 'ctx')), may hold values from -6 to 6
- cotangent: bfloat16 [32768, 768], P(('fsdp', 'ctx')), may hold values from -6 to 6
- lengths: int32 [4, 3], P('fsdp'), may hold values from 1024 to 5632, as said below
- norm_gain: bfloat16 [768], P('fsdp'), may hold values from 0.5 to 1.5
- gate_x_weight: bfloat16 [2, 768, 1536], P(None, 'fsdp', 'tp'), may hold values from -0.21875 to 0.21875
- state_weight: bfloat16 [768, 256], P('fsdp'), may hold values from -0.21875 to 0.21875
- step_weight: bfloat16 [768, 24], P('fsdp', 'tp'), may hold values from -0.21875 to 0.21875
- conv_heads: bfloat16 [24, 5, 64], P('tp', None, 'fsdp'), may hold values from -0.59765625 to 0.59765625
- conv_state: bfloat16 [5, 256], P(None, 'fsdp'), may hold values from -0.59765625 to 0.59765625
- step_bias: float32 [24], P('tp'), may hold values from -9 to -4
- decay_log: float32 [24], P('tp'), may hold values from -2 to 0.5
- skip_gain: float32 [24], P('tp'), may hold values from 0.5 to 1.5
- inner_gain: bfloat16 [24, 64], P('tp', 'fsdp'), may hold values from 0.5 to 1.5
- out_weight: bfloat16 [1536, 768], P('tp', 'fsdp'), may hold values from -0.15625 to 0.15625
Outputs:
- mixed: bfloat16 [32768, 768], P(('fsdp', 'ctx'), 'tp')
- input_grad: float32 [32768, 768], P(('fsdp', 'ctx'), 'tp')
- grad_norm_gain: float32 [768], P('fsdp')
- grad_gate_x_weight: float32 [2, 768, 1536], P(None, 'fsdp', 'tp')
- grad_state_weight: float32 [768, 256], P('fsdp')
- grad_step_weight: float32 [768, 24], P('fsdp', 'tp')
- grad_conv_heads: float32 [24, 5, 64], P('tp', None, 'fsdp')
- grad_conv_state: float32 [5, 256], P(None, 'fsdp')
- grad_step_bias: float32 [24], P('tp')
- grad_decay_log: float32 [24], P('tp')
- grad_skip_gain: float32 [24], P('tp')
- grad_inner_gain: float32 [24, 64], P('tp', 'fsdp')
- grad_out_weight: float32 [1536, 768], P('tp', 'fsdp')
The draws below stay inside these ranges and needn't reach their ends.
Inputs may be any that keep to these rules, and one draw needn't show every extreme that they name: Each group holds a ragged sequence, then a long one of 5632 positions, then a ragged one; the two ragged lengths sum to 2560 and each lies in 1024 to 1536.
All inputs are finite; a program needn't handle non-finite values.
Results may differ from the reference program's by a relative error of at most 0.018.
Values may be sent and summed in bfloat16 or wider, within the bound.
No kernel may reach another device: no remote copies, remote signals or barrier semaphores. Data moves between devices by JAX's collectives and lax.ppermute only.
A program may use at most 192 MiB of HBM per device.

```python
from functools import partial
import jax
import jax.numpy as jnp
from jax import lax

D = 768
HEADS = 24
HEADDIM = 64
STATE = 128
CONV = 4
BLOCK = 256
TOK_DEV = 2048
MINLEN = 1024
INNER = 1536
GROUP_TOK = 8192
GROUPS = 4
TOKENS = 32768


def draw_lengths(key, part):
    key = jax.random.fold_in(key, 7)
    spare_tokens = TOK_DEV // 4
    offsets = jax.random.randint(key, (GROUPS,), 0, spare_tokens + 1, dtype=jnp.int32)
    first_len = MINLEN + offsets
    last_len = MINLEN + spare_tokens - offsets
    long_len = jnp.full((GROUPS,), GROUP_TOK - 2 * MINLEN - spare_tokens, jnp.int32)
    return jnp.stack([first_len, long_len, last_len], axis=1).astype(jnp.int32)


def block_scale(own_key, extent, cuts, smallest, high):
    factor_of = 1.0
    for position, parts in cuts:
        steps = jax.random.uniform(jax.random.fold_in(jax.random.fold_in(own_key, 6), position), (parts,), jnp.float32, smallest / len(cuts), high / len(cuts))
        factor_of = factor_of * jnp.repeat(jnp.exp(steps), extent[position] // parts).reshape((-1,) + (1,) * (len(extent) - 1 - position))
    return factor_of


def centred(stream_key, extent, scale, reach, cuts=(), kind=jnp.bfloat16):
    values = scale * jax.random.normal(stream_key, extent, jnp.float32)
    if cuts:
        values = values * block_scale(stream_key, extent, cuts, -0.22, 0.18)
    return jnp.clip(values, -reach, reach).astype(kind)


def setup_inputs(seed: int = 0) -> dict:
    splits = jax.random.split(jax.random.key(seed), 15)
    tokens = centred(splits[0], (TOKENS, D), 1.0, 6.0, ((0, 16),))
    cotangent = centred(splits[1], (TOKENS, D), 1.0, 6.0, ((0, 16),))
    lengths = draw_lengths(jax.random.fold_in(splits[14], 71), 0)
    norm_gain = jnp.clip(1.0 + 0.1 * jax.random.normal(splits[3], (D,), jnp.float32), 0.5, 1.5).astype(jnp.bfloat16)
    gate_x_weight = centred(splits[4], (2, D, INNER), D ** -0.5, 0.21875, ((1, 4), (2, 2)))
    state_weight = centred(splits[5], (D, 2 * STATE), D ** -0.5, 0.21875, ((0, 4),))
    step_weight = centred(splits[6], (D, HEADS), D ** -0.5, 0.21875, ((0, 4), (1, 2)))
    conv_heads = jnp.clip(jax.random.uniform(splits[7], (HEADS, CONV + 1, HEADDIM), jnp.float32, -0.59765625, 0.59765625) * block_scale(splits[7], (HEADS, CONV + 1, HEADDIM), ((0, 2), (2, 4)), -0.4, 0.0), -0.59765625, 0.59765625).astype(jnp.bfloat16)
    conv_state = jnp.clip(jax.random.uniform(splits[8], (CONV + 1, 2 * STATE), jnp.float32, -0.59765625, 0.59765625) * block_scale(splits[8], (CONV + 1, 2 * STATE), ((1, 4),), -0.4, 0.0), -0.59765625, 0.59765625).astype(jnp.bfloat16)
    step_bias = jnp.clip(-9.0 + 5.0 * jax.random.uniform(splits[9], (HEADS,), jnp.float32) ** block_scale(splits[9], (HEADS,), ((0, 2),), -0.2, 0.2), -9.0, -4.0)
    decay_log = jnp.clip(-2.0 + 2.5 * jax.random.uniform(splits[10], (HEADS,), jnp.float32) ** block_scale(splits[10], (HEADS,), ((0, 2),), -0.2, 0.2), -2.0, 0.5)
    skip_gain = jnp.clip(0.5 + 1.0 * jax.random.uniform(splits[11], (HEADS,), jnp.float32) ** block_scale(splits[11], (HEADS,), ((0, 2),), -0.2, 0.2), 0.5, 1.5)
    inner_gain = jnp.clip(1.0 + 0.1 * jax.random.normal(splits[12], (HEADS, HEADDIM), jnp.float32), 0.5, 1.5).astype(jnp.bfloat16)
    out_weight = centred(splits[13], (INNER, D), INNER ** -0.5, 0.15625, ((0, 2), (1, 4)))
    return {"tokens": tokens, "cotangent": cotangent, "lengths": lengths, "norm_gain": norm_gain, "gate_x_weight": gate_x_weight, "state_weight": state_weight, "step_weight": step_weight, "conv_heads": conv_heads, "conv_state": conv_state, "step_bias": step_bias, "decay_log": decay_log, "skip_gain": skip_gain, "inner_gain": inner_gain, "out_weight": out_weight}


epsilon = 1e-05
highest = lax.Precision.HIGHEST

@jax.custom_vjp
def low(v):
    return lax.optimization_barrier(v.astype(jnp.bfloat16)).astype(jnp.float32)

@jax.custom_vjp
def low_back(v):
    return v

def low_keep(v):
    return (low(v), None)

def low_pass(kept, grad):
    return (grad,)

def back_keep(v):
    return (v, None)

def back_low(kept, grad):
    return (low(grad),)
low.defvjp(low_keep, low_pass)
low_back.defvjp(back_keep, back_low)

def multiply(formula, left_side, right_side):
    return jnp.einsum(formula, left_side, right_side, precision=highest, preferred_element_type=jnp.float32)

def convolve(extended, conv_taps, seg_ext, inner_width, state_width):
    margin = conv_taps.shape[0] - 2
    length = extended.shape[0] - margin
    current = seg_ext[margin:]
    running = jnp.zeros((length, extended.shape[1]), jnp.float32) + conv_taps[margin + 1]
    for lagging in range(margin + 1):
        window = extended[margin - lagging:margin - lagging + length]
        same_seq = (seg_ext[margin - lagging:margin - lagging + length] == current).astype(jnp.float32)
        running = running + conv_taps[lagging] * window * same_seq[:, None]
    activated = jax.nn.silu(running)
    return (low(activated[:, :inner_width]), low(activated[:, inner_width:inner_width + state_width]), low(activated[:, inner_width + state_width:]))

def ssd_block(skip_gain, entering, pieces):
    inputs, b_matrix, c_matrix, step_sizes, log_decay, seg_block, seg_before = pieces
    cumulative = jnp.cumsum(log_decay, axis=-1)
    order = jnp.arange(seg_block.shape[1], dtype=jnp.int32)
    causal = order[:, None] >= order[None, :]
    same_mask = ((seg_block[:, :, None] == seg_block[:, None, :]) & causal[None]).astype(jnp.float32)[:, None]
    spread = cumulative[..., :, None] - cumulative[..., None, :]
    decay = jnp.exp(jnp.where(same_mask > 0, spread, 0.0)) * same_mask
    gram = low_back(multiply('bin,bjn->bij', c_matrix, b_matrix))
    mixing = low(gram[:, None] * decay * step_sizes[:, :, None, :])
    inner_part = multiply('bhij,bhjp->bhip', mixing, inputs)
    keep_mask = (seg_block == seg_before[:, None]).astype(jnp.float32)
    c_scaled = low(c_matrix[:, None] * (jnp.exp(cumulative) * keep_mask[:, None])[..., None])
    outer_part = multiply('bhin,bhpn->bhip', c_scaled, low(entering))
    ssd_out = low_back(inner_part + outer_part + skip_gain[None, :, None, None] * inputs)
    tail_mask = (seg_block == seg_block[:, -1:]).astype(jnp.float32)
    scaled = low(inputs * (step_sizes * jnp.exp(cumulative[..., -1:] - cumulative) * tail_mask[:, None, :])[..., None])
    deltas = low_back(multiply('bhjp,bjn->bhpn', scaled, b_matrix))
    carried = jnp.exp(cumulative[..., -1]) * (seg_block[:, -1] == seg_before).astype(jnp.float32)[:, None]
    return (carried[:, :, None, None] * entering + deltas, ssd_out)

def forward(source, norm_gain, gate_x_weight, state_weight, step_weight, conv_heads, conv_state, step_bias, decay_log, skip_gain, inner_gain, out_weight, seg_ext, seg_prev):
    scale_rows = lax.rsqrt(lax.optimization_barrier(jnp.mean(source * source, axis=1, keepdims=True)) + epsilon)
    normed = low(source * scale_rows * norm_gain)
    gate_pre = low_back(multiply('td,de->te', normed, gate_x_weight[0]))
    mixed_x = low_back(low(multiply('td,de->te', normed, gate_x_weight[1])))
    bc_raw = low_back(low(multiply('td,de->te', normed, state_weight)))
    rate_raw = low_back(multiply('td,de->te', normed, step_weight))
    conv_in = jnp.concatenate([mixed_x, bc_raw], axis=1).reshape(GROUPS, GROUP_TOK, INNER + 2 * STATE)
    conv_ext = jnp.concatenate([jnp.zeros((GROUPS, CONV - 1, INNER + 2 * STATE), jnp.float32), conv_in], axis=1)
    conv_taps = jnp.concatenate([conv_heads.transpose(1, 0, 2).reshape(CONV + 1, INNER), conv_state], axis=1)
    x_part, b_part, c_part = jax.vmap(partial(convolve, inner_width=INNER, state_width=STATE), in_axes=(0, None, 0))(conv_ext, conv_taps, seg_ext)
    step_sizes = jax.nn.softplus(rate_raw + step_bias)
    log_decay = step_sizes * -jnp.exp(decay_log)
    blocks_total = GROUP_TOK // BLOCK
    inputs = x_part.reshape(GROUPS, blocks_total, BLOCK, HEADS, HEADDIM).transpose(1, 0, 3, 2, 4)
    b_blocks = b_part.reshape(GROUPS, blocks_total, BLOCK, STATE).transpose(1, 0, 2, 3)
    c_blocks = c_part.reshape(GROUPS, blocks_total, BLOCK, STATE).transpose(1, 0, 2, 3)
    step_blocks = step_sizes.reshape(GROUPS, blocks_total, BLOCK, HEADS).transpose(1, 0, 3, 2)
    decay_blocks = log_decay.reshape(GROUPS, blocks_total, BLOCK, HEADS).transpose(1, 0, 3, 2)
    seg_blocks = seg_ext[:, CONV - 1:].reshape(GROUPS, blocks_total, BLOCK).transpose(1, 0, 2)
    start_state = jnp.zeros((GROUPS, HEADS, HEADDIM, STATE), jnp.float32)
    block_step = jax.checkpoint(partial(ssd_block, skip_gain))
    final_state, outputs = lax.scan(block_step, start_state, (inputs, b_blocks, c_blocks, step_blocks, decay_blocks, seg_blocks, seg_prev.T))
    ssd_flat = outputs.transpose(1, 0, 3, 2, 4).reshape(TOKENS, INNER)
    gated = ssd_flat * jax.nn.silu(gate_pre)
    gate_scale = lax.rsqrt(lax.optimization_barrier(jnp.mean(gated * gated, axis=1, keepdims=True)) + epsilon)
    branch = low(gated * gate_scale * inner_gain.reshape(INNER))
    return source + multiply('te,ed->td', branch, out_weight)

def reference(tokens, cotangent, lengths, norm_gain, gate_x_weight, state_weight, step_weight, conv_heads, conv_state, step_bias, decay_log, skip_gain, inner_gain, out_weight):
    starts = jnp.cumsum(lengths, axis=1) - lengths
    place = jnp.arange(GROUP_TOK + CONV - 1, dtype=jnp.int32) - (CONV - 1)
    seg_ext = lax.optimization_barrier(jnp.sum((starts[:, None, :] <= place[None, :, None]).astype(jnp.int32), axis=2, dtype=jnp.int32)) - 1
    seg_prev = seg_ext[:, CONV - 2:CONV - 2 + GROUP_TOK].reshape(GROUPS, GROUP_TOK // BLOCK, BLOCK)[:, :, 0]
    floats = (tokens.astype(jnp.float32), norm_gain.astype(jnp.float32), gate_x_weight.astype(jnp.float32), state_weight.astype(jnp.float32), step_weight.astype(jnp.float32), conv_heads.astype(jnp.float32), conv_state.astype(jnp.float32), step_bias.astype(jnp.float32), decay_log.astype(jnp.float32), skip_gain.astype(jnp.float32), inner_gain.astype(jnp.float32), out_weight.astype(jnp.float32))
    result, pullback = jax.vjp(lambda *params: forward(*params, seg_ext, seg_prev), *floats)
    grads = pullback(cotangent.astype(jnp.float32))
    return (result.astype(jnp.bfloat16), grads[0], grads[1], grads[2], grads[3], grads[4], grads[5], grads[6], grads[7], grads[8], grads[9], grads[10], grads[11])
```

```python
import functools

import jax
import jax.numpy as jnp
from jax import lax
from jax.experimental import pallas as pl
from jax.experimental.pallas import tpu as pltpu
from jax.sharding import PartitionSpec as P

CONV = 4
BLOCK = 256
GROUP = 16
EPS = 1e-05

f32 = jnp.float32
bf16 = jnp.bfloat16


def contract(a, b, left, right):
    return lax.dot_general(a, b, (((left,), (right,)), ((), ())), preferred_element_type=f32)


def dot(a, b):
    return contract(a, b, 1, 0)


def dot_nt(a, b):
    return contract(a, b, 1, 1)


def dot_tn(a, b):
    return contract(a, b, 0, 0)


def spread_heads(values, selector, group):
    high = values.astype(bf16)
    low = (values - high.astype(f32)).astype(bf16)
    lane = lax.broadcasted_iota(jnp.int32, values.shape, 1)
    both = jnp.where(lane < GROUP * (group + 1), high.astype(f32), low.astype(f32)).astype(bf16)
    return dot(both, selector)


def sum_heads(values, selector):
    high = values.astype(bf16)
    low = (values - high.astype(f32)).astype(bf16)
    return dot_nt(high, selector) + dot_nt(low, selector)


def exact_dot(zero_one, values):
    high = values.astype(bf16)
    rest = values - high.astype(f32)
    mid = rest.astype(bf16)
    low = (rest - mid.astype(f32)).astype(bf16)
    return dot(zero_one, high) + dot(zero_one, mid) + dot(zero_one, low)


def sigmoid(v):
    return 0.5 * jnp.tanh(0.5 * v) + 0.5


def seg_of(sc, place):
    total = jnp.zeros_like(place) - 1
    for s in range(sc.shape[0] - 2):
        total = total + jnp.where(place >= sc[s], 1, 0)
    return total


def places(sc, block):
    return sc[sc.shape[0] - 2] + block * BLOCK


def column_iota():
    return lax.broadcasted_iota(jnp.int32, (BLOCK, 1), 0)


def row_iota():
    return lax.broadcasted_iota(jnp.int32, (1, BLOCK), 1)


def lag_masks(sc, block):
    place = places(sc, block) + column_iota()
    seg = seg_of(sc, place)
    return [jnp.where(seg_of(sc, place - k) == seg, 1.0, 0.0) for k in range(1, CONV)]


def lead_masks(sc, block):
    place = places(sc, block) + column_iota()
    seg = seg_of(sc, place)
    return [jnp.where(seg_of(sc, place + k) == seg, 1.0, 0.0) for k in range(1, CONV)]


def edges(sc, block):
    first = places(sc, block)
    return seg_of(sc, first - 1), seg_of(sc, first + BLOCK - 1)


def front(
    sc, tok, halo, gain, wxs, wst, taps, hp, e_step,
    normed, conv_in, x_out, xs_out, bc_out, rates, entering, lead, carry_out, last_state, last_decay,
    ext, state, total,
):
    block = pl.program_id(0)
    inner = x_out.shape[1]

    def project(values):
        wide = values.astype(f32)
        scale = lax.rsqrt(jnp.mean(wide * wide, axis=1, keepdims=True) + EPS)
        rows = (wide * scale * gain[...]).astype(bf16)
        return rows, dot(rows, wxs[...]).astype(bf16)

    @pl.when(block == 0)
    def _():
        ext[0:8, :] = project(halo[...])[1].astype(f32)[8:16]
        state[...] = jnp.zeros_like(state)
        total[...] = jnp.ones_like(total)

    @pl.when(block > 0)
    def _():
        ext[0:8, :] = ext[BLOCK : BLOCK + 8, :]

    rows, raw = project(tok[...])
    normed[...] = rows
    conv_in[...] = raw
    ext[8 : BLOCK + 8, :] = raw.astype(f32)
    pre = taps[CONV : CONV + 1, :] + taps[0:1, :] * raw.astype(f32)
    for k, mask in enumerate(lag_masks(sc, block), 1):
        pre = pre + taps[k : k + 1, :] * (ext[8 - k : BLOCK + 8 - k, :] * mask)
    post = (pre * sigmoid(pre)).astype(bf16)
    x_out[...] = post[:, :inner]
    bc_out[...] = post[:, inner:]
    rate = dot(rows, wst[...]) + hp[0:1, :]
    small = jnp.exp(-jnp.abs(rate))
    series = small * (1.0 - small * (0.5 - small * (1.0 / 3.0)))
    step = jnp.maximum(rate, 0.0) + jnp.where(small < 0.01, series, jnp.log(1.0 + small))
    inverse = 1.0 / (1.0 + small)
    slope = jnp.where(rate >= 0, inverse, small * inverse)
    lower = jnp.where(column_iota() >= row_iota(), 1.0, 0.0).astype(bf16)
    cum = exact_dot(lower, step * hp[1:2, :])
    lane = lax.broadcasted_iota(jnp.int32, cum.shape, 1)
    rates[...] = jnp.where(lane < 2 * GROUP, step, jnp.where(lane < 4 * GROUP, cum, slope))
    seg_before, seg_last = edges(sc, block)
    seg = seg_of(sc, places(sc, block) + column_iota())
    cum_last = cum[BLOCK - 1 : BLOCK, :]
    tail = jnp.exp(cum_last - cum) * jnp.where(seg == seg_last, 1.0, 0.0)
    x_step = post[:, :inner].astype(f32) * spread_heads(step, e_step[...], 0)
    xs_out[...] = x_step.astype(bf16)
    scaled = (x_step * spread_heads(tail, e_step[...], 0)).astype(bf16)
    delta = dot_tn(post[:, inner : inner + 128], scaled)
    keep = jnp.where(seg_last == seg_before, 1.0, 0.0)
    carried = jnp.exp(cum_last) * keep
    carried = spread_heads(jnp.broadcast_to(carried, (8, 128)), e_step[...], 0)
    carry_out[...] = carried
    entering[0] = state[...]
    lead[...] = total[...]
    state[...] = carried[0:1, :] * state[...] + delta
    total[...] = carried * total[...]

    @pl.when(block == pl.num_programs(0) - 1)
    def _():
        last_state[...] = state[...].astype(bf16)
        last_decay[...] = total[...]


def lane_halves():
    lane = lax.broadcasted_iota(jnp.int32, (1, 128), 1)
    first = jnp.where(lane < 64, 1.0, 0.0)
    return first.astype(bf16), (1.0 - first).astype(bf16)


def intra(sc, x, xs, bc, rates, skip, y_out):
    block = pl.program_id(0)
    pairs = x.shape[1] // 128
    first = places(sc, block)
    same = seg_of(sc, first + column_iota()) == seg_of(sc, first + row_iota())
    mask = same & (column_iota() >= row_iota())
    gram = jnp.where(mask, dot_nt(bc[:, 128:], bc[:, :128]), 0.0)
    across = rates[...].T
    left, right = lane_halves()
    for pair in range(pairs):
        at = slice(128 * pair, 128 * pair + 128)
        mixing = []
        for half in range(2):
            h = 2 * GROUP + 2 * pair + half
            decay = jnp.exp(jnp.minimum(rates[:, h : h + 1] - across[h : h + 1, :], 0.0))
            mixing.append((gram * decay).astype(bf16))
        values = xs[:, at]
        stacked = jnp.concatenate([values * left, values * right], axis=0)
        y_out[:, at] = dot(jnp.concatenate(mixing, axis=1), stacked) + skip[
            0:1, at
        ] * x[:, at].astype(f32)


def exit_factor(sc, block, rates, e_cum):
    seg_before, _ = edges(sc, block)
    seg = seg_of(sc, places(sc, block) + column_iota())
    keep = jnp.where(seg == seg_before, 1.0, 0.0)
    lane = lax.broadcasted_iota(jnp.int32, rates.shape, 1)
    cum = jnp.where((lane >= 2 * GROUP) & (lane < 4 * GROUP), rates[...], 0.0)
    return spread_heads(jnp.exp(cum) * keep, e_cum[...], 2)


def gate(
    sc, y_in, entering, lead, incoming, bc, rates, normed, cot, wgo, inner_gain, e_cum,
    y_out, state_out, pre_out, weighted_out, own_out, send_out, stats,
):
    block = pl.program_id(0)
    inner = y_in.shape[1]
    half = own_out.shape[1]
    state = (entering[0] + lead[0:1, :] * incoming[...]).astype(bf16)
    state_out[0] = state
    y = y_in[...] + exit_factor(sc, block, rates, e_cum) * dot(bc[:, 128:], state)
    y_out[...] = y
    pre = dot(normed[...], wgo[:, :inner])
    pre_out[...] = pre
    gated = y * pre * sigmoid(pre)
    weighted = dot(cot[...], wgo[:, inner:]) * inner_gain[...]
    weighted_out[...] = weighted
    out = dot_nt((gated * inner_gain[...]).astype(bf16), wgo[:, inner:]).astype(bf16)
    first = sc[sc.shape[0] - 1] == 0
    own_out[...] = jnp.where(first, out[:, :half], out[:, half:])
    send_out[...] = jnp.where(first, out[:, half:], out[:, :half])
    squares = jnp.sum(gated * gated, axis=1, keepdims=True)
    stat = jnp.sum(weighted * gated, axis=1, keepdims=True)
    lane = lax.broadcasted_iota(jnp.int32, (BLOCK, 128), 1)
    both = jnp.where(lane == 0, squares, jnp.where(lane == 1, stat, 0.0))
    stats[...] = both.T[0:8, :]


def turned(values):
    return jnp.concatenate([values] * 16, axis=0).T


def gate_back(
    sc, y, pre_in, weighted, stats, stats_other, normed, cot, x, bc, rates, state, carry, inner_gain, e_cum,
    d_ssd_out, d_gate_out, grad_out, exits, after, d_c, sums, first_grad, first_decay,
    grad_sum, chain, total,
    *, blocks, inner_whole,
):
    step = pl.program_id(0)
    block = blocks - 1 - step
    inner = y.shape[1]

    @pl.when(step == 0)
    def _():
        chain[...] = jnp.zeros_like(chain)
        total[...] = jnp.ones_like(total)
        sums[...] = jnp.zeros_like(sums)
        grad_sum[...] = jnp.zeros_like(grad_sum)

    row_stats = turned(stats[...] + stats_other[...])
    scale = lax.rsqrt(row_stats[:, 0:1] * (1.0 / inner_whole) + EPS)
    stat = row_stats[:, 1:2] * (scale * scale * scale) * (1.0 / inner_whole)
    pre = pre_in[...]
    sig = sigmoid(pre)
    act = pre * sig
    gated = y[...] * act
    scaled = gated * scale
    d_gated = scale * weighted[...] - gated * stat
    d_ssd = (d_gated * act).astype(bf16)
    d_gate = (d_gated * y[...] * (sig + act * (1.0 - sig))).astype(bf16)
    d_ssd_out[...] = d_ssd
    d_gate_out[...] = d_gate
    grad_sum[:, :inner] += dot_tn(normed[...], d_gate)
    grad_sum[:, inner:] += dot_tn(cot[...], (scaled * inner_gain[...]).astype(bf16))
    wide = d_ssd.astype(f32)
    sums[0:1, :] += jnp.sum(weighted[...] * scaled, axis=0, keepdims=True)
    sums[1:2, :] += jnp.sum(wide * x[...].astype(f32), axis=0, keepdims=True)
    d_exit = (wide * exit_factor(sc, block, rates, e_cum)).astype(bf16)
    d_c[...] = dot_nt(d_exit, state[0])
    exits[0] = chain[...]
    after[...] = total[...]
    chain[...] = carry[0:1, :] * chain[...] + dot_tn(bc[:, 128:], d_exit)
    total[...] = carry[...] * total[...]

    @pl.when(step == blocks - 1)
    def _():
        grad_out[...] = grad_sum[...].astype(bf16)
        first_grad[...] = chain[...].astype(bf16)
        first_decay[...] = total[...]


def intra_back(
    sc, d_ssd, xs, bc, rates, d_c_in, tok, own, other, stats, stats_other,
    d_xs, d_bc, mixed,
    *, inner_whole,
):
    block = pl.program_id(0)
    pairs = xs.shape[1] // 128
    first = places(sc, block)
    same = seg_of(sc, first + column_iota()) == seg_of(sc, first + row_iota())
    mask = same & (column_iota() <= row_iota())
    gram = jnp.where(mask, dot_nt(bc[:, :128], bc[:, 128:]), 0.0)
    across = rates[...].T
    left, right = lane_halves()
    d_gram = jnp.zeros((BLOCK, BLOCK), f32)
    for pair in range(pairs):
        at = slice(128 * pair, 128 * pair + 128)
        grads = d_ssd[:, at]
        halves = [grads * left, grads * right]
        mixing = []
        for half in range(2):
            h = 2 * GROUP + 2 * pair + half
            decay = jnp.exp(jnp.minimum(across[h : h + 1, :] - rates[:, h : h + 1], 0.0))
            mixing.append((gram * decay).astype(bf16))
            d_gram = d_gram + dot_nt(xs[:, at], halves[half]) * decay
        d_xs[:, at] = dot(jnp.concatenate(mixing, axis=1), jnp.concatenate(halves, axis=0))
    d_gram = jnp.where(mask, d_gram, 0.0).astype(bf16)
    d_bc[:, :128] = dot(d_gram, bc[:, 128:])
    d_bc[:, 128:] = dot_tn(d_gram, bc[:, :128]) + d_c_in[...]
    row_stats = turned(stats[...] + stats_other[...])
    scale = lax.rsqrt(row_stats[:, 0:1] * (1.0 / inner_whole) + EPS)
    half = mixed.shape[1]
    is_first = sc[sc.shape[0] - 1] == 0
    wide = tok[...].astype(f32)
    source = jnp.where(is_first, wide[:, :half], wide[:, half:])
    mixed[...] = (source + scale * (own[...].astype(f32) + other[...].astype(f32))).astype(bf16)


def conv_pre(sc, block, ext, taps):
    u = ext[8 : BLOCK + 8, :]
    masks = lag_masks(sc, block)
    windows = [u] + [ext[8 - k : BLOCK + 8 - k, :] * masks[k - 1] for k in range(1, CONV)]
    pre = taps[CONV : CONV + 1, :] + taps[0:1, :] * u
    for k in range(1, CONV):
        pre = pre + taps[k : k + 1, :] * windows[k]
    return pre, windows


def silu_slope(pre):
    sig = sigmoid(pre)
    return sig * (1.0 + pre * (1.0 - sig))


def scan_back(
    sc, d_xs_in, d_ssd, x, xs, y, bc, d_bc, rates, state, exits, after, reach, carry, hp, skip, e_step, e_cum,
    conv_in, halo, taps,
    d_pre, own_bc, send_bc, d_rate_out, sums, tap_sums,
    ext,
):
    block = pl.program_id(0)

    @pl.when(block == 0)
    def _():
        sums[...] = jnp.zeros_like(sums)
        tap_sums[...] = jnp.zeros_like(tap_sums)
        ext[0:8, :] = halo[...].astype(f32)[8:16]

    @pl.when(block > 0)
    def _():
        ext[0:8, :] = ext[BLOCK : BLOCK + 8, :]

    ext[8 : BLOCK + 8, :] = conv_in[...].astype(f32)
    _, seg_last = edges(sc, block)
    seg = seg_of(sc, places(sc, block) + column_iota())
    leaving = exits[0] + after[0:1, :] * reach[...]
    leaving_low = leaving.astype(bf16)
    lane = lax.broadcasted_iota(jnp.int32, rates.shape, 1)
    in_cum = (lane >= 2 * GROUP) & (lane < 4 * GROUP)
    cum = jnp.where(in_cum, rates[...], 0.0)
    tail = jnp.exp(cum[BLOCK - 1 : BLOCK, :] - cum) * jnp.where(seg == seg_last, 1.0, 0.0)
    tail = spread_heads(tail, e_cum[...], 2)
    xs_wide = xs[...].astype(f32)
    x_wide = x[...].astype(f32)
    d_wide = d_ssd[...].astype(f32)
    d_tail = tail * dot(bc[:, :128], leaving_low)
    d_b = d_bc[:, :128] + dot_nt((xs_wide * tail).astype(bf16), leaving_low)
    d_c = d_bc[:, 128:]
    is_first = sc[sc.shape[0] - 1] == 0
    own_bc[...] = jnp.where(is_first, d_b, d_c).astype(bf16)
    send_bc[...] = jnp.where(is_first, d_c, d_b).astype(bf16)
    d_xs = d_xs_in[...] + d_tail
    step = spread_heads(jnp.where(lane < 2 * GROUP, rates[...], 0.0), e_step[...], 0)
    d_x = d_xs * step + skip[0:1, :] * d_wide
    d_step = sum_heads(d_xs * x_wide, e_step[...])
    d_cum = sum_heads(d_wide * (y[...] - skip[0:1, :] * x_wide) - xs_wide * d_xs, e_step[...])
    at_last = jnp.sum(xs_wide * d_tail, axis=0, keepdims=True) + carry[0:1, :] * jnp.sum(
        leaving * state[0].astype(f32), axis=0, keepdims=True
    )
    at_last = sum_heads(jnp.broadcast_to(at_last, (8, at_last.shape[1])), e_step[...])[0:1, :]
    d_cum = d_cum + jnp.where(column_iota() == BLOCK - 1, at_last, 0.0)
    upper = jnp.where(column_iota() <= row_iota(), 1.0, 0.0).astype(bf16)
    d_decay = exact_dot(upper, d_cum) * hp[1:2, :]
    slope = pltpu.roll(rates[...], 128 - 4 * GROUP, 1)
    d_rate = jnp.where(lane < GROUP, (d_step + d_decay) * slope, 0.0)
    d_rate_out[...] = d_rate.astype(bf16)
    sums[0:1, :] += jnp.sum(d_rate, axis=0, keepdims=True)
    sums[1:2, :] += jnp.sum(jnp.where(lane < GROUP, d_decay * rates[...], 0.0), axis=0, keepdims=True)
    pre, windows = conv_pre(sc, block, ext, taps)
    grad = d_x * silu_slope(pre)
    d_pre[...] = grad.astype(bf16)
    for k in range(CONV):
        tap_sums[k : k + 1, :] += jnp.sum(grad * windows[k], axis=0, keepdims=True)
    tap_sums[CONV : CONV + 1, :] += jnp.sum(grad, axis=0, keepdims=True)


def bc_back(sc, own, other, conv_in, halo, taps, d_pre, tap_sums, ext):
    block = pl.program_id(0)

    @pl.when(block == 0)
    def _():
        tap_sums[...] = jnp.zeros_like(tap_sums)
        ext[0:8, :] = halo[...].astype(f32)[8:16]

    @pl.when(block > 0)
    def _():
        ext[0:8, :] = ext[BLOCK : BLOCK + 8, :]

    ext[8 : BLOCK + 8, :] = conv_in[...].astype(f32)
    pre, windows = conv_pre(sc, block, ext, taps)
    grad = (own[...].astype(f32) + other[...].astype(f32)) * silu_slope(pre)
    d_pre[...] = grad.astype(bf16)
    for k in range(CONV):
        tap_sums[k : k + 1, :] += jnp.sum(grad * windows[k], axis=0, keepdims=True)
    tap_sums[CONV : CONV + 1, :] += jnp.sum(grad, axis=0, keepdims=True)


def weights_back(
    sc, d_pre, d_pre_next, d_pre_bc, d_pre_bc_next, after, d_rate, normed, taps,
    d_conv_out, grad_out,
    grad_sum, ext,
    *, blocks,
):
    block = pl.program_id(0)
    inner = d_pre.shape[1]

    @pl.when(block == 0)
    def _():
        grad_sum[...] = jnp.zeros_like(grad_sum)

    ext[0:BLOCK, :inner] = d_pre[...].astype(f32)
    ext[0:BLOCK, inner:] = d_pre_bc[...].astype(f32)

    @pl.when(block == blocks - 1)
    def _():
        ext[BLOCK : BLOCK + 8, :] = after[...].astype(f32)[0:8]

    @pl.when(block < blocks - 1)
    def _():
        ext[BLOCK : BLOCK + 8, :inner] = d_pre_next[...].astype(f32)[0:8]
        ext[BLOCK : BLOCK + 8, inner:] = d_pre_bc_next[...].astype(f32)[0:8]

    grad = taps[0:1, :] * ext[0:BLOCK, :]
    for k, mask in enumerate(lead_masks(sc, block), 1):
        grad = grad + taps[k : k + 1, :] * (ext[k : BLOCK + k, :] * mask)
    low = jnp.concatenate([grad.astype(bf16), d_rate[...]], axis=1)
    d_conv_out[...] = low
    grad_sum[...] += dot_tn(normed[...], low)

    @pl.when(block == blocks - 1)
    def _():
        grad_out[...] = grad_sum[...].astype(bf16)


def input_back(sc, d_gate, d_conv, normed, w_gate, w_conv, own, send, stats):
    half = own.shape[1]
    grad = dot_nt(d_gate[...], w_gate[...]) + dot_nt(d_conv[...], w_conv[...])
    low = grad.astype(bf16)
    first = sc[sc.shape[0] - 1] == 0
    own[...] = jnp.where(first, low[:, :half], low[:, half:])
    send[...] = jnp.where(first, low[:, half:], low[:, :half])
    stat = jnp.sum(grad * normed[...].astype(f32), axis=1, keepdims=True)
    lane = lax.broadcasted_iota(jnp.int32, (BLOCK, 128), 1)
    stats[...] = jnp.where(lane == 0, stat, 0.0).T[0:8, :]


def finish(sc, tok, cot, gain, own, other, stats, stats_other, out):
    half = own.shape[1]
    width = tok.shape[1]
    first = sc[sc.shape[0] - 1] == 0

    def mine(values):
        return jnp.where(first, values[:, :half], values[:, half:])

    wide = tok[...].astype(f32)
    scale = lax.rsqrt(jnp.mean(wide * wide, axis=1, keepdims=True) + EPS)
    stat = turned(stats[...] + stats_other[...])[:, 0:1] * (1.0 / width)
    d_unit = mine(gain[...]) * (own[...].astype(f32) + other[...].astype(f32))
    unit = mine(wide) * scale
    out[...] = mine(cot[...].astype(f32)) + scale * (d_unit - unit * stat)


def run(body, blocks, inputs, outputs, scratch=(), flops=0, limit=48):
    def spec(shape, block, index):
        if block is None:
            rank = len(shape)
            return pl.BlockSpec(tuple(shape), lambda i: (0,) * rank)
        return pl.BlockSpec(block, index)

    in_specs = [pl.BlockSpec(memory_space=pltpu.SMEM)]
    in_specs += [spec(a.shape, block, index) for a, block, index in inputs[1:]]
    moved = sum(a.size * a.dtype.itemsize for a, _, _ in inputs[1:])
    moved += sum(functools.reduce(lambda p, q: p * q, s, 1) * jnp.dtype(d).itemsize for s, d, _, _ in outputs)
    return pl.pallas_call(
        body,
        grid=(blocks,),
        in_specs=in_specs,
        out_specs=[spec(s, block, index) for s, _, block, index in outputs],
        out_shape=[jax.ShapeDtypeStruct(s, d) for s, d, _, _ in outputs],
        scratch_shapes=list(scratch),
        compiler_params=pltpu.CompilerParams(
            dimension_semantics=("arbitrary",), vmem_limit_bytes=limit * 2**20
        ),
        cost_estimate=pl.CostEstimate(flops=flops, bytes_accessed=moved, transcendentals=0),
    )(*[a for a, _, _ in inputs])


def swap(array, axis, mask):
    size = lax.axis_size(axis)
    return lax.ppermute(array, axis, [(i, i ^ mask) for i in range(size)])


def shifted(array, axis, by):
    size = lax.axis_size(axis)
    return lax.ppermute(array, axis, [(i, i + by) for i in range(size) if 0 <= i + by < size])


def gather(array, axis):
    size = lax.axis_size(axis)
    place = lax.axis_index(axis)
    whole = jnp.zeros((size,) + array.shape, array.dtype)
    parts = [array] + [swap(array, axis, mask) for mask in range(1, size)]
    for mask, part in enumerate(parts):
        whole = lax.dynamic_update_index_in_dim(whole, part, jnp.bitwise_xor(place, mask), 0)
    return whole


def scattered_sum(chunks, axis):
    size = lax.axis_size(axis)
    place = lax.axis_index(axis)
    total = lax.dynamic_index_in_dim(chunks, place, 0, False).astype(f32)
    for mask in range(1, size):
        part = lax.dynamic_index_in_dim(chunks, jnp.bitwise_xor(place, mask), 0, False)
        total = total + swap(part, axis, mask).astype(f32)
    return total


def summed_over(array, axis):
    size = lax.axis_size(axis)
    place = lax.axis_index(axis)
    columns = array.shape[1]
    mask = 1
    while mask < size:
        columns //= 2
        upper = (place & mask) != 0
        low, high = array[:, :columns], array[:, columns:]
        sent = jnp.where(upper, low, high).astype(bf16)
        array = jnp.where(upper, high, low) + swap(sent, axis, mask).astype(f32)
        mask *= 2
    array = array.astype(bf16)
    while mask > 1:
        mask //= 2
        upper = (place & mask) != 0
        other = swap(array, axis, mask)
        array = jnp.concatenate(
            [jnp.where(upper, other, array), jnp.where(upper, array, other)], axis=1
        )
    return array


def reaching(state, decay, axis, direction):
    size = lax.axis_size(axis)
    high = decay.astype(bf16)
    low = (decay - high.astype(f32)).astype(bf16)
    by = 1
    total, factor = state.astype(f32), decay
    arrived, rest = jnp.zeros_like(total), None
    first = True
    while by < size or first:
        if first:
            sent = jnp.concatenate([state, high, low], axis=0)
        else:
            high = factor.astype(bf16)
            low = (factor - high.astype(f32)).astype(bf16)
            sent = jnp.concatenate([total.astype(bf16), high, low], axis=0)
        came = shifted(sent, axis, direction * by).astype(f32)
        rows = state.shape[0]
        came_state = came[:rows]
        came_factor = came[rows : rows + 8] + came[rows + 8 :]
        if first:
            arrived, rest = came_state, came_factor
            total, factor = factor[0:1] * came_state + total, factor * came_factor
            first = False
        else:
            arrived = arrived + rest[0:1] * came_state
            total, factor = total + factor[0:1] * came_state, factor * came_factor
            rest = rest * came_factor
        by *= 2
    return arrived


def per_device(
    tokens,
    cotangent,
    lengths,
    norm_gain,
    gate_x_weight,
    state_weight,
    step_weight,
    conv_heads,
    conv_state,
    step_bias,
    decay_log,
    skip_gain,
    inner_gain,
    out_weight,
):
    rows, width = tokens.shape
    shard = width // lax.axis_size("fsdp")
    heads = step_bias.shape[0]
    inner = out_weight.shape[0]
    head_size = inner // heads
    inner_whole = inner * lax.axis_size("tp")
    state_size = state_weight.shape[1] // 2
    blocks = rows // BLOCK
    half = width // 2
    fsdp_size = lax.axis_size("fsdp")
    place = lax.axis_index("fsdp")
    tp_rank = lax.axis_index("tp")
    conv_width = inner + 2 * state_size
    own_width = inner + state_size

    tokens_before = shifted(tokens[rows - 16 :], "ctx", 1)

    small = jnp.concatenate(
        [
            step_weight.reshape(-1),
            norm_gain,
            conv_heads.reshape(-1),
            conv_state.reshape(-1),
            inner_gain.reshape(-1),
        ]
    )
    small_rows = 16
    small = jnp.pad(small, (0, small_rows * conv_width - small.shape[0])).reshape(small_rows, conv_width)
    early = jnp.concatenate([jnp.concatenate([gate_x_weight[1], state_weight], axis=1), small], axis=0)
    early = gather(early, "fsdp")
    late = gather(jnp.concatenate([gate_x_weight[0], out_weight.T], axis=1), "fsdp")
    wgo = late.reshape(width, 2 * inner)
    wxs = early[:, :shard].reshape(width, conv_width)
    flat = early[:, shard:].reshape(fsdp_size, -1)

    def taken(start, count, shape):
        return flat[:, start : start + count].reshape((fsdp_size,) + shape), start + count

    step_full, at = taken(0, shard * heads, (shard, heads))
    norm_full, at = taken(at, shard, (shard,))
    conv_full, at = taken(at, conv_heads.size, conv_heads.shape)
    conv_state_full, at = taken(at, conv_state.size, conv_state.shape)
    inner_full, at = taken(at, inner_gain.size, inner_gain.shape)
    step_full = jnp.pad(step_full.reshape(width, heads), ((0, 0), (0, GROUP - heads)))
    wst = jnp.tile(step_full, (1, 128 // GROUP))
    gain = norm_full.reshape(1, width).astype(f32)
    taps_x = conv_full.transpose(2, 1, 0, 3).reshape(CONV + 1, inner)
    taps_bc = conv_state_full.transpose(1, 0, 2).reshape(CONV + 1, 2 * state_size)
    taps = jnp.pad(jnp.concatenate([taps_x, taps_bc], axis=1).astype(f32), ((0, 7 - CONV), (0, 0)))
    inner_row = inner_full.transpose(1, 0, 2).reshape(1, inner).astype(f32)
    own_bc_at = inner + state_size * tp_rank
    taps_own = lax.dynamic_slice_in_dim(taps, own_bc_at, state_size, 1)

    per_head = jnp.stack([step_bias, -jnp.exp(decay_log), skip_gain])
    hp = jnp.tile(jnp.pad(per_head, ((0, 5), (0, GROUP - heads))), (1, 128 // GROUP))
    skip_row = jnp.broadcast_to(jnp.repeat(skip_gain, head_size)[None], (8, inner))
    lane = jnp.arange(128, dtype=jnp.int32)[:, None]
    head = jnp.arange(inner, dtype=jnp.int32)[None, :] // head_size
    at_head = (lane % GROUP) == head
    e_step = (at_head & (lane < 2 * GROUP)).astype(bf16)
    e_cum = (at_head & (lane >= 2 * GROUP) & (lane < 4 * GROUP)).astype(bf16)

    starts = jnp.cumsum(lengths[0]) - lengths[0]
    sc = jnp.concatenate(
        [starts, jnp.stack([lax.axis_index("ctx") * rows, tp_rank])]
    ).astype(jnp.int32)

    scalars = (sc, None, None)

    def by_row(array, back=False):
        block = (BLOCK, array.shape[1])
        return (array, block, (lambda i: (blocks - 1 - i, 0)) if back else (lambda i: (i, 0)))

    def whole(array):
        return (array, None, None)

    def lead_spec(array, back=False):
        block = (8, array.shape[1])
        return (array, block, (lambda i: (blocks - 1 - i, 0)) if back else (lambda i: (i, 0)))

    def state_spec(array, back=False):
        block = (1,) + array.shape[1:]
        return (array, block, (lambda i: (blocks - 1 - i, 0, 0)) if back else (lambda i: (i, 0, 0)))

    def stat_spec(array, back=False):
        block = (8, BLOCK)
        return (array, block, (lambda i: (0, blocks - 1 - i)) if back else (lambda i: (0, i)))

    def out_rows(columns, kind, back=False):
        index = (lambda i: (blocks - 1 - i, 0)) if back else (lambda i: (i, 0))
        return ((rows, columns), kind, (BLOCK, columns), index)

    def out_lead(back=False):
        index = (lambda i: (blocks - 1 - i, 0)) if back else (lambda i: (i, 0))
        return ((8 * blocks, inner), f32, (8, inner), index)

    def out_state(kind, back=False):
        index = (lambda i: (blocks - 1 - i, 0, 0)) if back else (lambda i: (i, 0, 0))
        return ((blocks, state_size, inner), kind, (1, state_size, inner), index)

    def out_whole(shape, kind):
        return (shape, kind, None, None)

    out_stats = ((8, rows), f32, (8, BLOCK), lambda i: (0, i))

    (
        normed, conv_in, x, xs, bc, rates, entering, lead, carry, last_state, last_decay,
    ) = run(
        front,
        blocks,
        [
            scalars, by_row(tokens), whole(tokens_before), whole(gain), whole(wxs), whole(wst),
            whole(taps), whole(hp), whole(e_step),
        ],
        [
            out_rows(width, bf16), out_rows(conv_width, bf16), out_rows(inner, bf16), out_rows(inner, bf16),
            out_rows(2 * state_size, bf16), out_rows(128, f32), out_state(f32), out_lead(), out_lead(),
            out_whole((state_size, inner), bf16), out_whole((8, inner), f32),
        ],
        [
            pltpu.VMEM((BLOCK + 8, conv_width), f32), pltpu.VMEM((state_size, inner), f32),
            pltpu.VMEM((8, inner), f32),
        ],
        flops=2 * rows * width * (conv_width + 128),
    )
    conv_before = shifted(conv_in[rows - 16 :], "ctx", 1)
    incoming = reaching(last_state, last_decay, "ctx", 1)

    (y_intra,) = run(
        intra,
        blocks,
        [scalars, by_row(x), by_row(xs), by_row(bc), by_row(rates), whole(skip_row)],
        [out_rows(inner, f32)],
        flops=2 * rows * BLOCK * inner * 4,
    )
    y, states, pre, weighted, own_out, send_out, stats = run(
        gate,
        blocks,
        [
            scalars, by_row(y_intra), state_spec(entering), lead_spec(lead), whole(incoming), by_row(bc),
            by_row(rates), by_row(normed), by_row(cotangent), whole(wgo), whole(inner_row), whole(e_cum),
        ],
        [
            out_rows(inner, f32), out_state(bf16), out_rows(inner, f32), out_rows(inner, f32),
            out_rows(half, bf16), out_rows(half, bf16), out_stats,
        ],
        flops=2 * rows * width * inner * 3,
    )
    stats_other = swap(stats, "tp", 1)
    other_out = swap(send_out, "tp", 1)

    (
        d_ssd, d_gate, grad_go, exits, after, d_c, gate_sums, first_grad, first_decay,
    ) = run(
        functools.partial(gate_back, blocks=blocks, inner_whole=inner_whole),
        blocks,
        [
            scalars, by_row(y, True), by_row(pre, True), by_row(weighted, True), stat_spec(stats, True),
            stat_spec(stats_other, True), by_row(normed, True), by_row(cotangent, True), by_row(x, True),
            by_row(bc, True), by_row(rates, True), state_spec(states, True), lead_spec(carry, True),
            whole(inner_row), whole(e_cum),
        ],
        [
            out_rows(inner, bf16, True), out_rows(inner, bf16, True), out_whole((width, 2 * inner), bf16),
            out_state(f32, True), out_lead(True), out_rows(state_size, f32, True), out_whole((8, inner), f32),
            out_whole((state_size, inner), bf16), out_whole((8, inner), f32),
        ],
        [
            pltpu.VMEM((width, 2 * inner), f32), pltpu.VMEM((state_size, inner), f32),
            pltpu.VMEM((8, inner), f32),
        ],
        flops=2 * rows * width * inner * 2,
    )
    reach = reaching(first_grad, first_decay, "ctx", -1)
    grad_go = scattered_sum(grad_go.reshape(fsdp_size, shard, 2 * inner), "fsdp")
    grad_go = summed_over(grad_go, "ctx").astype(f32)

    d_xs, d_bc, mixed = run(
        functools.partial(intra_back, inner_whole=inner_whole),
        blocks,
        [
            scalars, by_row(d_ssd), by_row(xs), by_row(bc), by_row(rates), by_row(d_c), by_row(tokens),
            by_row(own_out), by_row(other_out), stat_spec(stats), stat_spec(stats_other),
        ],
        [out_rows(inner, f32), out_rows(2 * state_size, f32), out_rows(half, bf16)],
        flops=2 * rows * BLOCK * inner * 8,
    )

    conv_x = (conv_in, (BLOCK, inner), lambda i: (i, 0))
    d_pre, own_bc, send_bc, d_rate, head_sums, tap_sums = run(
        scan_back,
        blocks,
        [
            scalars, by_row(d_xs), by_row(d_ssd), by_row(x), by_row(xs), by_row(y), by_row(bc), by_row(d_bc),
            by_row(rates), state_spec(states), state_spec(exits), lead_spec(after), whole(reach),
            lead_spec(carry), whole(hp), whole(skip_row), whole(e_step), whole(e_cum), conv_x,
            (conv_before, (16, inner), lambda i: (0, 0)), (taps, (8, inner), lambda i: (0, 0)),
        ],
        [
            out_rows(inner, bf16), out_rows(state_size, bf16), out_rows(state_size, bf16), out_rows(128, bf16),
            out_whole((8, 128), f32), out_whole((8, inner), f32),
        ],
        [pltpu.VMEM((BLOCK + 8, inner), f32)],
        flops=2 * rows * inner * 128 * 6,
    )
    other_bc = swap(send_bc, "tp", 1)
    conv_own = lax.dynamic_slice_in_dim(conv_in, own_bc_at, state_size, 1)
    before_own = lax.dynamic_slice_in_dim(conv_before, own_bc_at, state_size, 1)
    d_pre_bc, tap_sums_bc = run(
        bc_back,
        blocks,
        [scalars, by_row(own_bc), by_row(other_bc), by_row(conv_own), whole(before_own), whole(taps_own)],
        [out_rows(state_size, bf16), out_whole((8, state_size), f32)],
        [pltpu.VMEM((BLOCK + 8, state_size), f32)],
    )
    d_pre_after = shifted(jnp.concatenate([d_pre[:16], d_pre_bc[:16]], axis=1), "ctx", -1)

    def next_rows(array):
        return (array, (16, array.shape[1]), lambda i: (jnp.minimum(i + 1, blocks - 1) * (BLOCK // 16), 0))

    taps_mine = jnp.concatenate([taps[:, :inner], taps_own], axis=1)
    d_conv, grad_conv = run(
        functools.partial(weights_back, blocks=blocks),
        blocks,
        [
            scalars, by_row(d_pre), next_rows(d_pre), by_row(d_pre_bc), next_rows(d_pre_bc),
            whole(d_pre_after), by_row(d_rate), by_row(normed), whole(taps_mine),
        ],
        [out_rows(conv_width, bf16), out_whole((width, conv_width), bf16)],
        [pltpu.VMEM((width, conv_width), f32), pltpu.VMEM((BLOCK + 8, own_width), f32)],
        flops=2 * rows * width * conv_width,
    )

    row_sums = jnp.concatenate(
        [
            jnp.concatenate([tap_sums[: CONV + 1], tap_sums_bc[: CONV + 1]], axis=1),
            jnp.pad(gate_sums[:2], ((0, 0), (0, state_size))),
            jnp.pad(head_sums[:2].reshape(1, 256), ((0, 0), (0, own_width - 256))),
        ],
        axis=0,
    )
    row_sums = jnp.pad(row_sums, ((0, 0), (0, conv_width - own_width)))
    sums_high = row_sums.astype(bf16)
    sums_low = (row_sums - sums_high.astype(f32)).astype(bf16)
    sums_both = jnp.concatenate([sums_high, sums_low], axis=0)
    chunks = jnp.concatenate(
        [
            grad_conv.reshape(fsdp_size, shard, conv_width),
            jnp.broadcast_to(sums_both[None], (fsdp_size,) + sums_both.shape),
        ],
        axis=1,
    )
    grad_mine = summed_over(scattered_sum(chunks, "fsdp"), "ctx").astype(f32)

    w_own = lax.dynamic_slice_in_dim(wxs, own_bc_at, state_size, 1)
    w_conv = jnp.concatenate([wxs[:, :inner], w_own, wst[:, :GROUP], jnp.zeros((width, 128 - GROUP), bf16)], axis=1)
    own_in, send_in, in_stats = run(
        input_back,
        blocks,
        [
            scalars, by_row(d_gate), by_row(d_conv), by_row(normed), (wgo, (width, inner), lambda i: (0, 0)),
            whole(w_conv),
        ],
        [out_rows(half, bf16), out_rows(half, bf16), out_stats],
        flops=2 * rows * width * (inner + conv_width),
    )
    other_in = swap(send_in, "tp", 1)
    in_stats_other = swap(in_stats, "tp", 1)
    (input_grad,) = run(
        finish,
        blocks,
        [
            scalars, by_row(tokens), by_row(cotangent), whole(gain), by_row(own_in), by_row(other_in),
            stat_spec(in_stats), stat_spec(in_stats_other),
        ],
        [out_rows(half, f32)],
    )

    grad_gate, grad_out = grad_go[:, :inner], grad_go[:, inner:].T
    grad_x = grad_mine[:shard, :inner]
    grad_state_own = grad_mine[:shard, inner:own_width]
    grad_step = grad_mine[:shard, own_width : own_width + heads]
    totals = grad_mine[shard : shard + 8] + grad_mine[shard + 8 :]
    own_state_weight = lax.dynamic_slice_in_dim(state_weight, state_size * tp_rank, state_size, 1)
    gain_part = (
        jnp.sum(gate_x_weight[0].astype(f32) * grad_gate, axis=1)
        + jnp.sum(gate_x_weight[1].astype(f32) * grad_x, axis=1)
        + jnp.sum(own_state_weight.astype(f32) * grad_state_own, axis=1)
        + jnp.sum(step_weight.astype(f32) * grad_step, axis=1)
    )
    tail = jnp.concatenate(
        [
            grad_state_own,
            totals[: CONV + 1, inner:own_width],
            jnp.pad(gain_part, (0, -shard % state_size)).reshape(-1, state_size),
        ],
        axis=0,
    )
    tail_other = swap(tail, "tp", 1)
    is_first = tp_rank == 0
    pair = jnp.concatenate(
        [jnp.where(is_first, tail, tail_other), jnp.where(is_first, tail_other, tail)], axis=1
    )
    grad_state = pair[:shard]
    state_cols = conv_state.shape[1]
    grad_conv_state = lax.dynamic_slice_in_dim(pair[shard : shard + CONV + 1], place * state_cols, state_cols, 1)
    gain_sum = (tail + tail_other)[shard + CONV + 1 :].reshape(-1)[:shard]
    grad_norm = gain_sum / norm_gain.astype(f32)
    tap_total = totals[: CONV + 1, :inner].reshape(CONV + 1, heads, fsdp_size, head_size // fsdp_size)
    grad_conv_heads = lax.dynamic_index_in_dim(tap_total, place, 2, False).transpose(1, 0, 2)
    inner_total = totals[CONV + 1, :inner].reshape(heads, fsdp_size, head_size // fsdp_size)
    grad_inner = lax.dynamic_index_in_dim(inner_total, place, 1, False) / inner_gain.astype(f32)
    grad_skip = jnp.sum(totals[CONV + 2, :inner].reshape(heads, head_size), axis=1)
    grad_bias = totals[CONV + 3, :heads]
    grad_decay = totals[CONV + 3, 128 : 128 + heads]
    return (
        mixed,
        input_grad,
        grad_norm,
        jnp.stack([grad_gate, grad_x]),
        grad_state,
        grad_step,
        grad_conv_heads,
        grad_conv_state,
        grad_bias,
        grad_decay,
        grad_skip,
        grad_inner,
        grad_out,
    )


def solution(mesh):
    in_specs = (
        P(("fsdp", "ctx"), None),
        P(("fsdp", "ctx"), None),
        P("fsdp", None),
        P("fsdp"),
        P(None, "fsdp", "tp"),
        P("fsdp", None),
        P("fsdp", "tp"),
        P("tp", None, "fsdp"),
        P(None, "fsdp"),
        P("tp"),
        P("tp"),
        P("tp"),
        P("tp", "fsdp"),
        P("tp", "fsdp"),
    )
    out_specs = (
        P(("fsdp", "ctx"), "tp"),
        P(("fsdp", "ctx"), "tp"),
        P("fsdp"),
        P(None, "fsdp", "tp"),
        P("fsdp", None),
        P("fsdp", "tp"),
        P("tp", None, "fsdp"),
        P(None, "fsdp"),
        P("tp"),
        P("tp"),
        P("tp"),
        P("tp", "fsdp"),
        P("tp", "fsdp"),
    )
    return jax.shard_map(
        per_device, mesh=mesh, in_specs=in_specs, out_specs=out_specs, check_vma=False
    )
```

```python
import functools

import jax
import jax.numpy as jnp
from jax import lax
from jax.experimental import pallas as pl
from jax.experimental.pallas import tpu as pltpu
from jax.sharding import PartitionSpec as P

CONV = 4
BLOCK = 256
GROUP = 16
EPS = 1e-05
CHUNK = 256
GAIN_AT = 252

f32 = jnp.float32
bf16 = jnp.bfloat16


def contract(a, b, left, right):
    return lax.dot_general(a, b, (((left,), (right,)), ((), ())), preferred_element_type=f32)


def dot(a, b):
    return contract(a, b, 1, 0)


def dot_nt(a, b):
    return contract(a, b, 1, 1)


def dot_tn(a, b):
    return contract(a, b, 0, 0)


def sum_heads(values, selector):
    high = values.astype(bf16)
    low = (values - high.astype(f32)).astype(bf16)
    return dot_nt(high, selector) + dot_nt(low, selector)


def exact_dot(zero_one, values):
    high = values.astype(bf16)
    rest = values - high.astype(f32)
    mid = rest.astype(bf16)
    low = (rest - mid.astype(f32)).astype(bf16)
    return dot(zero_one, high) + dot(zero_one, mid) + dot(zero_one, low)


def sigmoid(v):
    return 0.5 * jnp.tanh(0.5 * v) + 0.5


def seg_of(sc, place):
    total = jnp.zeros_like(place) - 1
    for s in range(sc.shape[0] - 2):
        total = total + jnp.where(place >= sc[s], 1, 0)
    return total


def places(sc, block):
    return sc[sc.shape[0] - 2] + block * BLOCK


def column_iota():
    return lax.broadcasted_iota(jnp.int32, (BLOCK, 1), 0)


def row_iota():
    return lax.broadcasted_iota(jnp.int32, (1, BLOCK), 1)


def lag_masks(sc, block):
    place = places(sc, block) + column_iota()
    seg = seg_of(sc, place)
    return [jnp.where(seg_of(sc, place - k) == seg, 1.0, 0.0) for k in range(1, CONV)]


def lead_masks(sc, block):
    place = places(sc, block) + column_iota()
    seg = seg_of(sc, place)
    return [jnp.where(seg_of(sc, place + k) == seg, 1.0, 0.0) for k in range(1, CONV)]


def edges(sc, block):
    first = places(sc, block)
    return seg_of(sc, first - 1), seg_of(sc, first + BLOCK - 1)


def halves_of(values, group):
    high = values.astype(bf16)
    low = (values - high.astype(f32)).astype(bf16)
    lane = lax.broadcasted_iota(jnp.int32, values.shape, 1)
    return jnp.where(lane < GROUP * (group + 1), high.astype(f32), low.astype(f32)).astype(bf16)


def columns_of(width):
    return [slice(at, at + CHUNK) for at in range(0, width, CHUNK)]


def front(
    sc, tok, halo, gain, wxs, wst, taps, hp, e_step,
    normed, conv_x, conv_own, halo_x, halo_own, x_out, xs_out, bc_out, slope_x, slope_own,
    rates, entering, lead, carry_out, last_state, last_decay,
    ext, state, total,
):
    block = pl.program_id(0)
    inner = x_out.shape[1]
    states = bc_out.shape[1] // 2
    is_first = sc[sc.shape[0] - 1] == 0

    def mine(values):
        return jnp.where(is_first, values[:, :states], values[:, states:])

    def normalize(values):
        wide = values.astype(f32)
        scale = lax.rsqrt(jnp.mean(wide * wide, axis=1, keepdims=True) + EPS)
        return (wide * scale * gain[...]).astype(bf16)

    @pl.when(block == 0)
    def _():
        raw = dot(normalize(halo[...]), wxs[...]).astype(bf16)
        halo_x[...] = raw[:, :inner]
        halo_own[...] = mine(raw[:, inner:].astype(f32)).astype(bf16)
        ext[0:8, :] = raw.astype(f32)[8:16]
        state[...] = jnp.zeros_like(state)
        total[...] = jnp.ones_like(total)

    @pl.when(block > 0)
    def _():
        ext[0:8, :] = ext[BLOCK : BLOCK + 8, :]

    rows = normalize(tok[...])
    normed[...] = rows
    rate = dot(rows, wst[...]) + hp[0:1, :]
    small = jnp.exp(-jnp.abs(rate))
    series = small * (1.0 - small * (0.5 - small * (1.0 / 3.0)))
    step = jnp.maximum(rate, 0.0) + jnp.where(small < 0.01, series, jnp.log(1.0 + small))
    inverse = 1.0 / (1.0 + small)
    slope = jnp.where(rate >= 0, inverse, small * inverse)
    lower = jnp.where(column_iota() >= row_iota(), 1.0, 0.0).astype(bf16)
    cum = exact_dot(lower, step * hp[1:2, :])
    lane = lax.broadcasted_iota(jnp.int32, cum.shape, 1)
    rates[...] = jnp.where(lane < 2 * GROUP, step, jnp.where(lane < 4 * GROUP, cum, slope))
    seg_before, seg_last = edges(sc, block)
    seg = seg_of(sc, places(sc, block) + column_iota())
    cum_last = cum[BLOCK - 1 : BLOCK, :]
    tail = jnp.exp(cum_last - cum) * jnp.where(seg == seg_last, 1.0, 0.0)
    keep = jnp.where(seg_last == seg_before, 1.0, 0.0)
    carried = jnp.broadcast_to(jnp.exp(cum_last) * keep, (8, 128))
    carried = dot(halves_of(carried, 0), e_step[...])
    carry_out[...] = carried
    entering[0] = state[...]
    lead[...] = total[...]
    total[...] = carried * total[...]
    step_parts = halves_of(step, 0)
    tail_parts = halves_of(tail, 0)
    masks = lag_masks(sc, block)
    b_rows = None
    chunks = columns_of(inner + 2 * states)
    for at in chunks[-1:] + chunks[:-1]:
        raw = dot(rows, wxs[:, at]).astype(bf16)
        wide = raw.astype(f32)
        ext[8 : BLOCK + 8, at] = wide
        pre = taps[CONV : CONV + 1, at] + taps[0:1, at] * wide
        for k, mask in enumerate(masks, 1):
            pre = pre + taps[k : k + 1, at] * (ext[8 - k : BLOCK + 8 - k, at] * mask)
        sig = sigmoid(pre)
        act = pre * sig
        post = act.astype(bf16)
        turn = sig + act * (1.0 - sig)
        if at.start >= inner:
            bc_out[...] = post
            b_rows = post[:, :states]
            conv_own[...] = mine(wide).astype(bf16)
            slope_own[...] = mine(turn).astype(bf16)
        else:
            x_out[:, at] = post
            conv_x[:, at] = raw
            slope_x[:, at] = turn.astype(bf16)
            x_step = post.astype(f32) * dot(step_parts, e_step[:, at])
            xs_out[:, at] = x_step.astype(bf16)
            scaled = (x_step * dot(tail_parts, e_step[:, at])).astype(bf16)
            state[:, at] = carried[0:1, at] * state[:, at] + dot_tn(b_rows, scaled)

    @pl.when(block == pl.num_programs(0) - 1)
    def _():
        last_state[...] = state[...].astype(bf16)
        last_decay[...] = total[...]


def lane_halves():
    lane = lax.broadcasted_iota(jnp.int32, (1, 128), 1)
    first = jnp.where(lane < 64, 1.0, 0.0)
    return first.astype(bf16), (1.0 - first).astype(bf16)


def intra(sc, x, xs, bc, rates, skip, y_out):
    block = pl.program_id(0)
    pairs = x.shape[1] // 128
    first = places(sc, block)
    same = seg_of(sc, first + column_iota()) == seg_of(sc, first + row_iota())
    mask = same & (column_iota() >= row_iota())
    gram = jnp.where(mask, dot_nt(bc[:, 128:], bc[:, :128]), 0.0)
    across = rates[...].T
    left, right = lane_halves()
    for pair in range(pairs):
        at = slice(128 * pair, 128 * pair + 128)
        mixing = []
        for half in range(2):
            h = 2 * GROUP + 2 * pair + half
            decay = jnp.exp(jnp.minimum(rates[:, h : h + 1] - across[h : h + 1, :], 0.0))
            mixing.append((gram * decay).astype(bf16))
        values = xs[:, at]
        stacked = jnp.concatenate([values * left, values * right], axis=0)
        y_out[:, at] = dot(jnp.concatenate(mixing, axis=1), stacked) + skip[
            0:1, at
        ] * x[:, at].astype(f32)


def exit_parts(sc, block, rates):
    seg_before, _ = edges(sc, block)
    seg = seg_of(sc, places(sc, block) + column_iota())
    keep = jnp.where(seg == seg_before, 1.0, 0.0)
    lane = lax.broadcasted_iota(jnp.int32, rates.shape, 1)
    cum = jnp.where((lane >= 2 * GROUP) & (lane < 4 * GROUP), rates[...], 0.0)
    return halves_of(jnp.exp(cum) * keep, 2)


def gate_products(sc, normed, cot, wgo, inner_gain, pre, weighted):
    inner = pre.shape[1]
    for at in columns_of(inner):
        pre[:, at] = dot(normed[...], wgo[:, at]).astype(bf16)
        back = dot(cot[...], wgo[:, inner + at.start : inner + at.stop])
        weighted[:, at] = (back * inner_gain[:, at]).astype(bf16)


def gate(
    sc, y_in, entering, lead, incoming, bc, rates, pre_in, weighted, wo, inner_gain, e_cum,
    y_out, state_out, own_out, send_out, stats,
    turned_weight,
):
    block = pl.program_id(0)
    inner = y_in.shape[1]
    half = own_out.shape[1]

    @pl.when(block == 0)
    def _():
        turned_weight[...] = wo[...].T

    parts = exit_parts(sc, block, rates)
    squares = jnp.zeros((BLOCK, 1), f32)
    stat = jnp.zeros((BLOCK, 1), f32)
    out = jnp.zeros((BLOCK, 2 * half), f32)
    for at in columns_of(inner):
        state = (entering[0, :, at] + lead[0:1, at] * incoming[:, at]).astype(bf16)
        state_out[0, :, at] = state
        y = y_in[:, at] + dot(parts, e_cum[:, at]) * dot(bc[:, 128:], state)
        y_out[:, at] = y
        pre = pre_in[:, at].astype(f32)
        gated = y * pre * sigmoid(pre)
        squares = squares + jnp.sum(gated * gated, axis=1, keepdims=True)
        stat = stat + jnp.sum(weighted[:, at].astype(f32) * gated, axis=1, keepdims=True)
        out = out + dot((gated * inner_gain[:, at]).astype(bf16), turned_weight[at, :])
    out = out.astype(bf16)
    first = sc[sc.shape[0] - 1] == 0
    own_out[...] = jnp.where(first, out[:, :half], out[:, half:])
    send_out[...] = jnp.where(first, out[:, half:], out[:, :half])
    lane = lax.broadcasted_iota(jnp.int32, (BLOCK, 128), 1)
    both = jnp.where(lane == 0, squares, jnp.where(lane == 1, stat, 0.0))
    stats[...] = both.T[0:8, :]


def turned(values):
    return jnp.concatenate([values] * 16, axis=0).T


def gate_back(
    sc, y_in, pre_in, weighted_in, stats, stats_other, x, bc, rates, state, carry, inner_gain, e_cum,
    d_ssd_out, d_gate_out, branch_out, exits, after, d_c, sums, first_grad, first_decay,
    chain, total,
    *, blocks, inner_whole,
):
    step = pl.program_id(0)
    block = blocks - 1 - step
    inner = y_in.shape[1]

    @pl.when(step == 0)
    def _():
        chain[...] = jnp.zeros_like(chain)
        total[...] = jnp.ones_like(total)
        sums[...] = jnp.zeros_like(sums)

    row_stats = turned(stats[...] + stats_other[...])
    scale = lax.rsqrt(row_stats[:, 0:1] * (1.0 / inner_whole) + EPS)
    stat = row_stats[:, 1:2] * (scale * scale * scale) * (1.0 / inner_whole)
    parts = exit_parts(sc, block, rates)
    exits[0] = chain[...]
    after[...] = total[...]
    total[...] = carry[...] * total[...]
    grad_c = jnp.zeros(d_c.shape, f32)
    for at in columns_of(inner):
        y = y_in[:, at]
        pre = pre_in[:, at].astype(f32)
        sig = sigmoid(pre)
        act = pre * sig
        gated = y * act
        scaled = gated * scale
        weighted = weighted_in[:, at].astype(f32)
        d_gated = scale * weighted - gated * stat
        d_ssd = (d_gated * act).astype(bf16)
        d_ssd_out[:, at] = d_ssd
        d_gate_out[:, at] = (d_gated * y * (sig + act * (1.0 - sig))).astype(bf16)
        branch_out[:, at] = (scaled * inner_gain[:, at]).astype(bf16)
        wide = d_ssd.astype(f32)
        sums[0:1, at] += jnp.sum(weighted * scaled, axis=0, keepdims=True)
        sums[1:2, at] += jnp.sum(wide * x[:, at].astype(f32), axis=0, keepdims=True)
        d_exit = (wide * dot(parts, e_cum[:, at])).astype(bf16)
        grad_c = grad_c + dot_nt(d_exit, state[0, :, at])
        chain[:, at] = carry[0:1, at] * chain[:, at] + dot_tn(bc[:, 128:], d_exit)
    d_c[...] = grad_c

    @pl.when(step == blocks - 1)
    def _():
        first_grad[...] = chain[...].astype(bf16)
        first_decay[...] = total[...]


def gate_grads(
    sc, normed, cot, d_gate, branch, w_gate, out, gain_grad,
    across, *, steps, row_parts, column_parts,
):
    step = pl.program_id(0)

    @pl.when(step == 0)
    def _():
        across[...] = normed[...].T
        gain_grad[...] = jnp.zeros_like(gain_grad)

    @pl.when(step == steps)
    def _():
        across[...] = cot[...].T

    def store(grad):
        rows = out.shape[3]
        low = grad.astype(bf16)
        for f in range(row_parts):
            for c in range(column_parts):
                at = (f * column_parts + c) * rows
                out[f, c, 0] = low[at : at + rows]

    @pl.when(step < steps)
    def _():
        grad = dot(across[...], d_gate[...])
        store(grad)
        total = jnp.sum(grad * w_gate[...].astype(f32), axis=1, keepdims=True)
        gain_grad[...] += jnp.broadcast_to(total, gain_grad.shape)

    @pl.when(step >= steps)
    def _():
        store(dot(across[...], branch[...]))


def intra_back(sc, d_ssd, xs, bc, rates, d_c_in, d_xs, d_bc):
    block = pl.program_id(0)
    pairs = xs.shape[1] // 128
    first = places(sc, block)
    same = seg_of(sc, first + column_iota()) == seg_of(sc, first + row_iota())
    mask = same & (column_iota() <= row_iota())
    gram = jnp.where(mask, dot_nt(bc[:, :128], bc[:, 128:]), 0.0)
    across = rates[...].T
    left, right = lane_halves()
    d_gram = jnp.zeros((BLOCK, BLOCK), f32)
    for pair in range(pairs):
        at = slice(128 * pair, 128 * pair + 128)
        grads = d_ssd[:, at]
        halves = [grads * left, grads * right]
        mixing = []
        for half in range(2):
            h = 2 * GROUP + 2 * pair + half
            decay = jnp.exp(jnp.minimum(across[h : h + 1, :] - rates[:, h : h + 1], 0.0))
            mixing.append((gram * decay).astype(bf16))
            d_gram = d_gram + dot_nt(xs[:, at], halves[half]) * decay
        d_xs[:, at] = dot(jnp.concatenate(mixing, axis=1), jnp.concatenate(halves, axis=0))
    d_gram = jnp.where(mask, d_gram, 0.0).astype(bf16)
    d_bc[:, :128] = dot(d_gram, bc[:, 128:])
    d_bc[:, 128:] = dot_tn(d_gram, bc[:, :128]) + d_c_in[...]


def output(sc, tok, own, other, stats, stats_other, mixed, *, inner_whole):
    row_stats = turned(stats[...] + stats_other[...])
    scale = lax.rsqrt(row_stats[:, 0:1] * (1.0 / inner_whole) + EPS)
    half = mixed.shape[1]
    is_first = sc[sc.shape[0] - 1] == 0
    wide = tok[...].astype(f32)
    source = jnp.where(is_first, wide[:, :half], wide[:, half:])
    mixed[...] = (source + scale * (own[...].astype(f32) + other[...].astype(f32))).astype(bf16)


def tap_grads(sc, block, sums, at, grad, ext, masks):
    sums[CONV : CONV + 1, at] += jnp.sum(grad, axis=0, keepdims=True)
    sums[0:1, at] += jnp.sum(grad * ext[8 : BLOCK + 8, at], axis=0, keepdims=True)
    for k, mask in enumerate(masks, 1):
        window = ext[8 - k : BLOCK + 8 - k, at] * mask
        sums[k : k + 1, at] += jnp.sum(grad * window, axis=0, keepdims=True)


def scan_back(
    sc, d_xs_in, d_ssd, x, xs, y, bc, d_bc, rates, state, exits, after, reach, carry, hp, skip, e_step, e_cum,
    conv_in, halo, slope_x,
    d_pre, own_bc, send_bc, d_rate_out, sums, tap_sums,
    ext,
):
    block = pl.program_id(0)

    @pl.when(block == 0)
    def _():
        sums[...] = jnp.zeros_like(sums)
        tap_sums[...] = jnp.zeros_like(tap_sums)
        ext[0:8, :] = halo[...].astype(f32)[8:16]

    @pl.when(block > 0)
    def _():
        ext[0:8, :] = ext[BLOCK : BLOCK + 8, :]

    _, seg_last = edges(sc, block)
    seg = seg_of(sc, places(sc, block) + column_iota())
    masks = lag_masks(sc, block)
    lane = lax.broadcasted_iota(jnp.int32, rates.shape, 1)
    in_cum = (lane >= 2 * GROUP) & (lane < 4 * GROUP)
    cum = jnp.where(in_cum, rates[...], 0.0)
    tail = jnp.exp(cum[BLOCK - 1 : BLOCK, :] - cum) * jnp.where(seg == seg_last, 1.0, 0.0)
    tail_parts = halves_of(tail, 2)
    step_parts = halves_of(jnp.where(lane < 2 * GROUP, rates[...], 0.0), 0)
    d_b = d_bc[:, :128]
    d_step = jnp.zeros((BLOCK, 128), f32)
    d_cum = jnp.zeros((BLOCK, 128), f32)
    at_last = jnp.zeros((8, 128), f32)
    for at in columns_of(d_pre.shape[1]):
        heads = e_step[:, at]
        ext[8 : BLOCK + 8, at] = conv_in[:, at].astype(f32)
        leaving = exits[0, :, at] + after[0:1, at] * reach[:, at]
        leaving_low = leaving.astype(bf16)
        factor = dot(tail_parts, e_cum[:, at])
        xs_wide = xs[:, at].astype(f32)
        x_wide = x[:, at].astype(f32)
        d_wide = d_ssd[:, at].astype(f32)
        d_tail = factor * dot(bc[:, :128], leaving_low)
        d_b = d_b + dot_nt((xs_wide * factor).astype(bf16), leaving_low)
        d_xs = d_xs_in[:, at] + d_tail
        skipped = skip[0:1, at]
        d_x = d_xs * dot(step_parts, heads) + skipped * d_wide
        d_step = d_step + dot_nt((d_xs * x_wide).astype(bf16), heads)
        d_cum = d_cum + sum_heads(d_wide * (y[:, at] - skipped * x_wide) - xs_wide * d_xs, heads)
        last = jnp.sum(xs_wide * d_tail, axis=0, keepdims=True) + carry[0:1, at] * jnp.sum(
            leaving * state[0, :, at].astype(f32), axis=0, keepdims=True
        )
        at_last = at_last + sum_heads(jnp.broadcast_to(last, (8, CHUNK)), heads)
        grad = d_x * slope_x[:, at].astype(f32)
        d_pre[:, at] = grad.astype(bf16)
        tap_grads(sc, block, tap_sums, at, grad, ext, masks)
    d_c = d_bc[:, 128:]
    is_first = sc[sc.shape[0] - 1] == 0
    own_bc[...] = jnp.where(is_first, d_b, d_c).astype(bf16)
    send_bc[...] = jnp.where(is_first, d_c, d_b).astype(bf16)
    d_cum = d_cum + jnp.where(column_iota() == BLOCK - 1, at_last[0:1, :], 0.0)
    upper = jnp.where(column_iota() <= row_iota(), 1.0, 0.0).astype(bf16)
    d_decay = exact_dot(upper, d_cum) * hp[1:2, :]
    slope = pltpu.roll(rates[...], 128 - 4 * GROUP, 1)
    d_rate = jnp.where(lane < GROUP, (d_step + d_decay) * slope, 0.0)
    d_rate_out[...] = d_rate.astype(bf16)
    sums[0:1, :] += jnp.sum(d_rate, axis=0, keepdims=True)
    sums[1:2, :] += jnp.sum(jnp.where(lane < GROUP, d_decay * rates[...], 0.0), axis=0, keepdims=True)


def conv_back(
    sc, d_pre, d_pre_next, own, other, slope, own_next, other_next, slope_next,
    after_x, after_own, after_other, after_slope, conv_in, halo, d_rate, taps,
    d_conv, tap_sums,
    lead, ext,
    *, blocks,
):
    block = pl.program_id(0)
    inner = d_pre.shape[1]
    last = block == blocks - 1

    @pl.when(block == 0)
    def _():
        tap_sums[...] = jnp.zeros_like(tap_sums)
        ext[0:8, :] = halo[...].astype(f32)[8:16]

    @pl.when(block > 0)
    def _():
        ext[0:8, :] = ext[BLOCK : BLOCK + 8, :]

    ext[8 : BLOCK + 8, :] = conv_in[...].astype(f32)
    grad_own = (own[...].astype(f32) + other[...].astype(f32)) * slope[...].astype(f32)
    tap_grads(sc, block, tap_sums, slice(0, own.shape[1]), grad_own, ext, lag_masks(sc, block))
    lead[0:BLOCK, :inner] = d_pre[...].astype(f32)
    lead[0:BLOCK, inner:] = grad_own

    @pl.when(last)
    def _():
        lead[BLOCK : BLOCK + 8, :inner] = after_x[...].astype(f32)[0:8]
        sums = (after_own[...].astype(f32) + after_other[...].astype(f32)) * after_slope[...].astype(f32)
        lead[BLOCK : BLOCK + 8, inner:] = sums[0:8]

    @pl.when(jnp.logical_not(last))
    def _():
        lead[BLOCK : BLOCK + 8, :inner] = d_pre_next[...].astype(f32)[0:8]
        sums = (own_next[...].astype(f32) + other_next[...].astype(f32)) * slope_next[...].astype(f32)
        lead[BLOCK : BLOCK + 8, inner:] = sums[0:8]

    masks = lead_masks(sc, block)
    for start in range(0, lead.shape[1], 128):
        at = slice(start, start + 128)
        grad = taps[0:1, at] * lead[0:BLOCK, at]
        for k, mask in enumerate(masks, 1):
            grad = grad + taps[k : k + 1, at] * (lead[k : BLOCK + k, at] * mask)
        d_conv[:, at] = grad.astype(bf16)
    d_conv[:, lead.shape[1] :] = d_rate[...]


def conv_grads(sc, normed, d_conv, w_conv, gain_in, small, out, across, gain_grad, *, steps, row_parts):
    step = pl.program_id(0)

    @pl.when(step == 0)
    def _():
        across[...] = normed[...].T
        gain_grad[...] = gain_in[...]

    grad = dot(across[...], d_conv[...])
    gain_grad[...] += jnp.broadcast_to(
        jnp.sum(grad * w_conv[...].astype(f32), axis=1, keepdims=True), gain_grad.shape
    )
    total = gain_grad[:, 0:1]
    high = total.astype(bf16).astype(f32)
    lane = lax.broadcasted_iota(jnp.int32, grad.shape, 1)
    lane = jnp.where(step == steps - 1, lane, 0)
    grad = jnp.where(lane == GAIN_AT, high, jnp.where(lane == GAIN_AT + 1, total - high, grad))
    low = grad.astype(bf16)
    rows = grad.shape[0] // row_parts
    for f in range(row_parts):
        out[f, 0, :rows] = low[f * rows : (f + 1) * rows]
        out[f, 0, rows:] = small[...]


def input_back(sc, d_gate, d_conv, normed, w_gate, w_conv, own, send, stats, turned_gate, turned_conv):
    half = own.shape[1]

    @pl.when(pl.program_id(0) == 0)
    def _():
        turned_gate[...] = w_gate[...].T
        turned_conv[...] = w_conv[...].T

    first = sc[sc.shape[0] - 1] == 0
    grad = dot(d_gate[...], turned_gate[...]) + dot(d_conv[...], turned_conv[...])
    low = grad.astype(bf16)
    own[...] = jnp.where(first, low[:, :half], low[:, half:])
    send[...] = jnp.where(first, low[:, half:], low[:, :half])
    stat = jnp.sum(grad * normed[...].astype(f32), axis=1, keepdims=True)
    lane = lax.broadcasted_iota(jnp.int32, (BLOCK, 128), 1)
    stats[...] = jnp.where(lane == 0, stat, 0.0).T[0:8, :]


def finish(sc, tok, cot, gain, own, other, stats, stats_other, out):
    half = own.shape[1]
    width = tok.shape[1]
    first = sc[sc.shape[0] - 1] == 0

    def mine(values):
        return jnp.where(first, values[:, :half], values[:, half:])

    wide = tok[...].astype(f32)
    scale = lax.rsqrt(jnp.mean(wide * wide, axis=1, keepdims=True) + EPS)
    stat = turned(stats[...] + stats_other[...])[:, 0:1] * (1.0 / width)
    d_unit = mine(gain[...]) * (own[...].astype(f32) + other[...].astype(f32))
    unit = mine(wide) * scale
    out[...] = mine(cot[...].astype(f32)) + scale * (d_unit - unit * stat)


def run(body, blocks, inputs, outputs, scratch=(), micros=1, limit=48):
    def spec(shape, block, index):
        if block is None:
            rank = len(shape)
            return pl.BlockSpec(tuple(shape), lambda i: (0,) * rank)
        return pl.BlockSpec(block, index)

    in_specs = [pl.BlockSpec(memory_space=pltpu.SMEM)]
    in_specs += [spec(a.shape, block, index) for a, block, index in inputs[1:]]
    moved = sum(a.size * a.dtype.itemsize for a, _, _ in inputs[1:])
    moved += sum(functools.reduce(lambda p, q: p * q, s, 1) * jnp.dtype(d).itemsize for s, d, _, _ in outputs)
    return pl.pallas_call(
        body,
        grid=(blocks,),
        in_specs=in_specs,
        out_specs=[spec(s, block, index) for s, _, block, index in outputs],
        out_shape=[jax.ShapeDtypeStruct(s, d) for s, d, _, _ in outputs],
        scratch_shapes=list(scratch),
        compiler_params=pltpu.CompilerParams(
            dimension_semantics=("arbitrary",), vmem_limit_bytes=limit * 2**20
        ),
        cost_estimate=pl.CostEstimate(flops=micros * 10**9, bytes_accessed=moved, transcendentals=0),
    )(*[a for a, _, _ in inputs])


def swap(array, axis, mask):
    size = lax.axis_size(axis)
    return lax.ppermute(array, axis, [(i, i ^ mask) for i in range(size)])


def shifted(array, axis, by):
    size = lax.axis_size(axis)
    return lax.ppermute(array, axis, [(i, i + by) for i in range(size) if 0 <= i + by < size])


def crossed(array):
    size = lax.axis_size("ctx")
    cores = lax.axis_size("tp")
    pairs = [
        (i * cores + core, (i - 1) * cores + cores - 1 - core)
        for i in range(1, size)
        for core in range(cores)
    ]
    return lax.ppermute(array, ("ctx", "tp"), pairs)


def exchanged(array, axis):
    return [swap(array, axis, mask) for mask in range(1, lax.axis_size(axis))]


def placed(parts, axis):
    size = lax.axis_size(axis)
    place = lax.axis_index(axis)
    whole = jnp.zeros((size,) + parts[0].shape, parts[0].dtype)
    for mask, part in enumerate(parts):
        whole = lax.dynamic_update_index_in_dim(whole, part, jnp.bitwise_xor(place, mask), 0)
    return whole


def scatter_parts(chunks, axis):
    size = lax.axis_size(axis)
    place = lax.axis_index(axis)
    parts = [lax.dynamic_index_in_dim(chunks, place, 0, False)]
    for mask in range(1, size):
        part = lax.dynamic_index_in_dim(chunks, jnp.bitwise_xor(place, mask), 0, False)
        parts.append(swap(part, axis, mask))
    return parts


def total_of(parts):
    total = parts[0].astype(f32)
    for part in parts[1:]:
        total = total + part.astype(f32)
    return total


def following(arrays, *others):
    flat, tree = jax.tree.flatten(arrays)
    held = lax.optimization_barrier(tuple(flat) + tuple(others))
    return jax.tree.unflatten(tree, held[: len(flat)])


def summed_over(array, axis):
    size = lax.axis_size(axis)
    place = lax.axis_index(axis)
    columns = array.shape[1]
    mask = 1
    while mask < size:
        columns //= 2
        upper = (place & mask) != 0
        low, high = array[:, :columns], array[:, columns:]
        sent = jnp.where(upper, low, high).astype(bf16)
        array = jnp.where(upper, high, low) + swap(sent, axis, mask).astype(f32)
        mask *= 2
    array = array.astype(bf16)
    while mask > 1:
        mask //= 2
        upper = (place & mask) != 0
        other = swap(array, axis, mask)
        array = jnp.concatenate(
            [jnp.where(upper, other, array), jnp.where(upper, array, other)], axis=1
        )
    return array


def reaching(state, decay, axis, direction, beside):
    size = lax.axis_size(axis)
    high = decay.astype(bf16)
    low = (decay - high.astype(f32)).astype(bf16)
    by = 1
    total, factor = state.astype(f32), decay
    arrived, rest = jnp.zeros_like(total), None
    first = True
    while by < size or first:
        if first:
            sent = jnp.concatenate([state, high, low], axis=0)
        else:
            high = factor.astype(bf16)
            low = (factor - high.astype(f32)).astype(bf16)
            sent = jnp.concatenate([total.astype(bf16), high, low], axis=0)
        came = shifted(sent, axis, direction * by)
        if first:
            came = following(came, beside)
        came = came.astype(f32)
        rows = state.shape[0]
        came_state = came[:rows]
        came_factor = came[rows : rows + 8] + came[rows + 8 :]
        if first:
            arrived, rest = came_state, came_factor
            total, factor = factor[0:1] * came_state + total, factor * came_factor
            first = False
        else:
            arrived = arrived + rest[0:1] * came_state
            total, factor = total + factor[0:1] * came_state, factor * came_factor
            rest = rest * came_factor
        by *= 2
    return arrived


def per_device(
    tokens,
    cotangent,
    lengths,
    norm_gain,
    gate_x_weight,
    state_weight,
    step_weight,
    conv_heads,
    conv_state,
    step_bias,
    decay_log,
    skip_gain,
    inner_gain,
    out_weight,
):
    rows, width = tokens.shape
    fsdp_size = lax.axis_size("fsdp")
    ctx_size = lax.axis_size("ctx")
    shard = width // fsdp_size
    heads = step_bias.shape[0]
    inner = out_weight.shape[0]
    head_size = inner // heads
    inner_whole = inner * lax.axis_size("tp")
    state_size = state_weight.shape[1] // 2
    blocks = rows // BLOCK
    half = width // 2
    place = lax.axis_index("fsdp")
    tp_rank = lax.axis_index("tp")
    is_first = tp_rank == 0
    conv_width = inner + 2 * state_size
    own_width = inner + state_size

    big = exchanged_first = jnp.concatenate([gate_x_weight[1], state_weight], axis=1)
    big_parts = [big] + exchanged(exchanged_first, "fsdp")
    tokens_before = shifted(tokens[rows - 16 :], "ctx", 1)
    small = jnp.concatenate(
        [
            step_weight.reshape(-1),
            norm_gain,
            conv_heads.reshape(-1),
            conv_state.reshape(-1),
            inner_gain.reshape(-1),
        ]
    )
    small = jnp.pad(small, (0, -small.shape[0] % 2048)).reshape(-1, 128)
    small = following(small, tokens_before)
    flat = placed([small] + exchanged(small, "fsdp"), "fsdp").reshape(fsdp_size, -1)
    wxs = placed(big_parts, "fsdp").reshape(width, conv_width)
    late = jnp.concatenate([gate_x_weight[0], out_weight.T], axis=1)
    late = following(late, wxs)
    late_parts = [late] + exchanged(late, "fsdp")

    def taken(start, count, shape):
        return flat[:, start : start + count].reshape((fsdp_size,) + shape), start + count

    step_full, at = taken(0, shard * heads, (shard, heads))
    norm_full, at = taken(at, shard, (shard,))
    conv_full, at = taken(at, conv_heads.size, conv_heads.shape)
    conv_state_full, at = taken(at, conv_state.size, conv_state.shape)
    inner_full, at = taken(at, inner_gain.size, inner_gain.shape)
    step_full = jnp.pad(step_full.reshape(width, heads), ((0, 0), (0, GROUP - heads)))
    wst = jnp.tile(step_full, (1, 128 // GROUP))
    gain = norm_full.reshape(1, width).astype(f32)
    taps_x = conv_full.transpose(2, 1, 0, 3).reshape(CONV + 1, inner)
    taps_bc = conv_state_full.transpose(1, 0, 2).reshape(CONV + 1, 2 * state_size)
    taps = jnp.pad(jnp.concatenate([taps_x, taps_bc], axis=1).astype(f32), ((0, 7 - CONV), (0, 0)))
    inner_row = inner_full.transpose(1, 0, 2).reshape(1, inner).astype(f32)

    per_head = jnp.stack([step_bias, -jnp.exp(decay_log), skip_gain])
    hp = jnp.tile(jnp.pad(per_head, ((0, 5), (0, GROUP - heads))), (1, 128 // GROUP))
    skip_row = jnp.broadcast_to(jnp.repeat(skip_gain, head_size)[None], (8, inner))
    lane = jnp.arange(128, dtype=jnp.int32)[:, None]
    head = jnp.arange(inner, dtype=jnp.int32)[None, :] // head_size
    at_head = (lane % GROUP) == head
    e_step = (at_head & (lane < 2 * GROUP)).astype(bf16)
    e_cum = (at_head & (lane >= 2 * GROUP) & (lane < 4 * GROUP)).astype(bf16)

    starts = jnp.cumsum(lengths[0]) - lengths[0]
    sc = jnp.concatenate(
        [starts, jnp.stack([lax.axis_index("ctx") * rows, tp_rank])]
    ).astype(jnp.int32)

    scalars = (sc, None, None)

    def by_row(array, back=False):
        block = (BLOCK, array.shape[1])
        return (array, block, (lambda i: (blocks - 1 - i, 0)) if back else (lambda i: (i, 0)))

    def whole(array):
        return (array, None, None)

    def lead_spec(array, back=False):
        block = (8, array.shape[1])
        return (array, block, (lambda i: (blocks - 1 - i, 0)) if back else (lambda i: (i, 0)))

    def state_spec(array, back=False):
        block = (1,) + array.shape[1:]
        return (array, block, (lambda i: (blocks - 1 - i, 0, 0)) if back else (lambda i: (i, 0, 0)))

    def stat_spec(array, back=False):
        block = (8, BLOCK)
        return (array, block, (lambda i: (0, blocks - 1 - i)) if back else (lambda i: (0, i)))

    def out_rows(columns, kind, back=False):
        index = (lambda i: (blocks - 1 - i, 0)) if back else (lambda i: (i, 0))
        return ((rows, columns), kind, (BLOCK, columns), index)

    def out_lead(back=False):
        index = (lambda i: (blocks - 1 - i, 0)) if back else (lambda i: (i, 0))
        return ((8 * blocks, inner), f32, (8, inner), index)

    def out_state(kind, back=False):
        index = (lambda i: (blocks - 1 - i, 0, 0)) if back else (lambda i: (i, 0, 0))
        return ((blocks, state_size, inner), kind, (1, state_size, inner), index)

    def out_whole(shape, kind):
        return (shape, kind, None, None)

    def next_rows(array):
        return (array, (16, array.shape[1]), lambda i: (jnp.minimum(i + 1, blocks - 1) * (BLOCK // 16), 0))

    out_stats = ((8, rows), f32, (8, BLOCK), lambda i: (0, i))

    (
        normed, conv_x, conv_own, halo_x, halo_own, x, xs, bc, slope_x, slope_own,
        rates, entering, lead, carry, last_state, last_decay,
    ) = run(
        front,
        blocks,
        [
            scalars, by_row(tokens), whole(tokens_before), whole(gain), whole(wxs), whole(wst),
            whole(taps), whole(hp), whole(e_step),
        ],
        [
            out_rows(width, bf16), out_rows(inner, bf16), out_rows(state_size, bf16),
            out_whole((16, inner), bf16), out_whole((16, state_size), bf16), out_rows(inner, bf16),
            out_rows(inner, bf16), out_rows(2 * state_size, bf16), out_rows(inner, bf16),
            out_rows(state_size, bf16), out_rows(128, f32), out_state(f32), out_lead(), out_lead(),
            out_whole((state_size, inner), bf16), out_whole((8, inner), f32),
        ],
        [
            pltpu.VMEM((BLOCK + 8, conv_width), f32), pltpu.VMEM((state_size, inner), f32),
            pltpu.VMEM((8, inner), f32),
        ],
        micros=20,
    )

    def intra_scan(operands):
        x, xs, bc, rates = operands
        return run(
            intra,
            blocks,
            [scalars, by_row(x), by_row(xs), by_row(bc), by_row(rates), whole(skip_row)],
            [out_rows(inner, f32)],
            micros=11,
        )[0]

    y_intra = intra_scan((x, xs, bc, rates))
    incoming = reaching(last_state, last_decay, "ctx", 1, y_intra)
    wgo = placed(following(late_parts, y_intra), "fsdp").reshape(width, 2 * inner)
    pre, weighted = run(
        gate_products,
        blocks,
        [scalars, by_row(normed), by_row(cotangent), whole(wgo), whole(inner_row)],
        [out_rows(inner, bf16), out_rows(inner, bf16)],
        micros=8,
    )
    incoming = following(incoming, pre)
    y, states, own_out, send_out, stats = run(
        gate,
        blocks,
        [
            scalars, by_row(y_intra), state_spec(entering), lead_spec(lead), whole(incoming), by_row(bc),
            by_row(rates), by_row(pre), by_row(weighted), (wgo, (width, inner), lambda i: (0, 1)),
            whole(inner_row), whole(e_cum),
        ],
        [
            out_rows(inner, f32), out_state(bf16), out_rows(half, bf16), out_rows(half, bf16), out_stats,
        ],
        [pltpu.VMEM((inner, width), bf16)],
        micros=12,
    )
    stats_other = swap(stats, "tp", 1)
    other_out = swap(following(send_out, stats_other), "tp", 1)

    (
        d_ssd, d_gate, branch, exits, after, d_c, gate_sums, first_grad, first_decay,
    ) = run(
        functools.partial(gate_back, blocks=blocks, inner_whole=inner_whole),
        blocks,
        [
            scalars, by_row(y, True), by_row(pre, True), by_row(weighted, True), stat_spec(stats, True),
            stat_spec(stats_other, True), by_row(x, True), by_row(bc, True), by_row(rates, True),
            state_spec(states, True), lead_spec(carry, True), whole(inner_row), whole(e_cum),
        ],
        [
            out_rows(inner, bf16, True), out_rows(inner, bf16, True), out_rows(inner, bf16, True),
            out_state(f32, True), out_lead(True), out_rows(state_size, f32, True), out_whole((8, inner), f32),
            out_whole((state_size, inner), bf16), out_whole((8, inner), f32),
        ],
        [pltpu.VMEM((state_size, inner), f32), pltpu.VMEM((8, inner), f32)],
        micros=12,
    )

    steps = inner // CHUNK
    row_parts, column_parts = fsdp_size, 4
    piece = shard // column_parts
    grad_go, gain_grad = run(
        functools.partial(gate_grads, steps=steps, row_parts=row_parts, column_parts=column_parts),
        2 * steps,
        [
            scalars, whole(normed), whole(cotangent),
            (d_gate, (rows, CHUNK), lambda i: (0, jnp.minimum(i, steps - 1))),
            (branch, (rows, CHUNK), lambda i: (0, jnp.maximum(i - steps, 0))),
            (wgo, (width, CHUNK), lambda i: (0, jnp.minimum(i, steps - 1))),
        ],
        [
            ((row_parts, column_parts, 2 * steps, piece, CHUNK), bf16,
             (row_parts, column_parts, 1, piece, CHUNK), lambda i: (0, 0, i, 0, 0)),
            out_whole((width, 128), f32),
        ],
        [pltpu.VMEM((width, rows), bf16)],
        micros=8,
    )
    reach = reaching(first_grad, first_decay, "ctx", -1, grad_go)
    go_parts = scatter_parts(grad_go, "fsdp")

    d_xs, d_bc = run(
        intra_back,
        blocks,
        [
            scalars, by_row(following(d_ssd, grad_go)), by_row(xs), by_row(bc), by_row(rates), by_row(d_c),
        ],
        [out_rows(inner, f32), out_rows(2 * state_size, f32)],
        micros=14,
    )
    reach = following(reach, d_xs)
    go_total = total_of(following(go_parts, d_xs)).astype(bf16)
    direct = ctx_size == column_parts
    go_parts = scatter_parts(go_total, "ctx") if direct else [go_total]

    d_pre, own_bc, send_bc, d_rate, head_sums, tap_sums = run(
        scan_back,
        blocks,
        [
            scalars, by_row(d_xs), by_row(d_ssd), by_row(x), by_row(xs), by_row(y), by_row(bc), by_row(d_bc),
            by_row(rates), state_spec(states), state_spec(exits), lead_spec(after), whole(reach),
            lead_spec(carry), whole(hp), whole(skip_row), whole(e_step), whole(e_cum), by_row(conv_x),
            whole(halo_x), by_row(slope_x),
        ],
        [
            out_rows(inner, bf16), out_rows(state_size, bf16), out_rows(state_size, bf16), out_rows(128, bf16),
            out_whole((8, 128), f32), out_whole((8, inner), f32),
        ],
        [pltpu.VMEM((BLOCK + 8, inner), f32)],
        micros=24,
    )
    other_bc = swap(send_bc, "tp", 1)
    after_both = shifted(jnp.concatenate([d_pre[:16], own_bc[:16], slope_own[:16]], axis=1), "ctx", -1)
    after_other = crossed(send_bc[:16])
    (mixed,) = run(
        functools.partial(output, inner_whole=inner_whole),
        blocks,
        [
            scalars, by_row(following(tokens, d_pre)), by_row(own_out), by_row(other_out), stat_spec(stats),
            stat_spec(stats_other),
        ],
        [out_rows(half, bf16)],
        micros=4,
    )
    other_bc, after_both, after_other = following((other_bc, after_both, after_other), mixed)
    own_bc_at = inner + state_size * tp_rank
    taps_own = lax.dynamic_slice_in_dim(taps, own_bc_at, state_size, 1)
    taps_mine = jnp.concatenate([taps[:, :inner], taps_own], axis=1)
    after_x = after_both[:, :inner]
    after_own = after_both[:, inner:own_width]
    after_slope = after_both[:, own_width:]
    d_conv, tap_sums_bc = run(
        functools.partial(conv_back, blocks=blocks),
        blocks,
        [
            scalars, by_row(d_pre), next_rows(d_pre), by_row(own_bc), by_row(other_bc), by_row(slope_own),
            next_rows(own_bc), next_rows(other_bc), next_rows(slope_own), whole(after_x), whole(after_own),
            whole(after_other), whole(after_slope), by_row(conv_own), whole(halo_own), by_row(d_rate),
            whole(taps_mine),
        ],
        [out_rows(conv_width, bf16), out_whole((8, state_size), f32)],
        [pltpu.VMEM((BLOCK + 8, own_width), f32), pltpu.VMEM((BLOCK + 8, state_size), f32)],
        micros=8,
    )

    if direct:
        go_total = total_of(following(go_parts, d_pre)).astype(bf16)
        go_parts = exchanged(go_total, "ctx")
    row_sums = jnp.concatenate(
        [
            jnp.concatenate([tap_sums[: CONV + 1], tap_sums_bc[: CONV + 1]], axis=1),
            jnp.pad(gate_sums[:2], ((0, 0), (0, state_size))),
            jnp.pad(head_sums[:2].reshape(1, 256), ((0, 0), (0, own_width - 256))),
        ],
        axis=0,
    )
    row_sums = jnp.pad(row_sums, ((0, 0), (0, conv_width - own_width)))
    sums_high = row_sums.astype(bf16)
    sums_low = (row_sums - sums_high.astype(f32)).astype(bf16)
    sums_both = jnp.concatenate([sums_high, sums_low], axis=0)
    w_own = lax.dynamic_slice_in_dim(wxs, own_bc_at, state_size, 1)
    w_conv = jnp.concatenate([wxs[:, :inner], w_own, wst[:, :GROUP], jnp.zeros((width, 128 - GROUP), bf16)], axis=1)
    steps = conv_width // CHUNK
    (grad_conv,) = run(
        functools.partial(conv_grads, steps=steps, row_parts=row_parts),
        steps,
        [
            scalars, whole(normed), (d_conv, (rows, CHUNK), lambda i: (0, i)),
            (w_conv, (width, CHUNK), lambda i: (0, i)), whole(gain_grad),
            (sums_both, (16, CHUNK), lambda i: (0, i)),
        ],
        [
            ((row_parts, steps, shard + 16, CHUNK), bf16, (row_parts, 1, shard + 16, CHUNK),
             lambda i: (0, i, 0, 0)),
        ],
        [pltpu.VMEM((width, rows), bf16), pltpu.VMEM((width, 128), f32)],
        micros=6,
    )
    conv_parts = scatter_parts(grad_conv, "fsdp")

    own_in, send_in, in_stats = run(
        input_back,
        blocks,
        [
            scalars, by_row(following(d_gate, grad_conv)), by_row(d_conv), by_row(normed),
            (wgo, (width, inner), lambda i: (0, 0)), whole(w_conv),
        ],
        [out_rows(half, bf16), out_rows(half, bf16), out_stats],
        [pltpu.VMEM((inner, width), bf16), pltpu.VMEM((conv_width, width), bf16)],
        micros=11,
    )
    other_in = swap(send_in, "tp", 1)
    in_stats_other = swap(in_stats, "tp", 1)
    conv_total = total_of(following(conv_parts, in_stats)).astype(bf16)
    conv_parts = scatter_parts(conv_total, "ctx") if direct else [conv_total]
    (input_grad,) = run(
        finish,
        blocks,
        [
            scalars, by_row(tokens), by_row(cotangent), whole(gain), by_row(own_in), by_row(other_in),
            stat_spec(in_stats), stat_spec(in_stats_other),
        ],
        [out_rows(half, f32)],
        micros=7,
    )
    if direct:
        conv_total = total_of(following(conv_parts, input_grad)).astype(bf16)
        conv_sum = placed([conv_total] + exchanged(conv_total, "ctx"), "ctx")
        go_sum = placed([go_total] + following(go_parts, d_conv), "ctx")
    else:
        conv_sum = summed_over(conv_parts[0].reshape(-1, CHUNK).astype(f32), "ctx").reshape(conv_total.shape)
        go_sum = summed_over(go_parts[0].reshape(-1, CHUNK).astype(f32), "ctx").reshape(go_total.shape)

    go_sum = go_sum.transpose(0, 2, 1, 3).reshape(shard, 2 * inner).astype(f32)
    grad_gate, grad_out = go_sum[:, :inner], go_sum[:, inner:].T
    last = conv_sum[steps - 1]
    last_other = swap(last, "tp", 1)
    grad_x = conv_sum[: steps - 1, :shard].transpose(1, 0, 2).reshape(shard, inner).astype(f32)
    totals = conv_sum[: steps - 1, shard:].astype(f32)
    totals = (totals[:, :8] + totals[:, 8:]).transpose(1, 0, 2).reshape(8, inner)
    grad_step = last[:shard, state_size : state_size + heads].astype(f32)
    pair = jnp.where(
        is_first,
        jnp.concatenate([last[:, :state_size], last_other[:, :state_size]], axis=1),
        jnp.concatenate([last_other[:, :state_size], last[:, :state_size]], axis=1),
    ).astype(f32)
    grad_state = pair[:shard]
    state_cols = conv_state.shape[1]
    state_taps = pair[shard : shard + CONV + 1] + pair[shard + 8 : shard + 8 + CONV + 1]
    grad_conv_state = lax.dynamic_slice_in_dim(state_taps, place * state_cols, state_cols, 1)
    gain_sum = last[:shard, GAIN_AT : GAIN_AT + 2].astype(f32) + last_other[:shard, GAIN_AT : GAIN_AT + 2].astype(f32)
    grad_norm = jnp.sum(gain_sum, axis=1) / norm_gain.astype(f32)
    tap_total = totals[: CONV + 1].reshape(CONV + 1, heads, fsdp_size, head_size // fsdp_size)
    grad_conv_heads = lax.dynamic_index_in_dim(tap_total, place, 2, False).transpose(1, 0, 2)
    inner_total = totals[CONV + 1].reshape(heads, fsdp_size, head_size // fsdp_size)
    grad_inner = lax.dynamic_index_in_dim(inner_total, place, 1, False) / inner_gain.astype(f32)
    grad_skip = jnp.sum(totals[CONV + 2].reshape(heads, head_size), axis=1)
    grad_bias = totals[CONV + 3, :heads]
    grad_decay = totals[CONV + 3, 128 : 128 + heads]
    return (
        mixed,
        input_grad,
        grad_norm,
        jnp.stack([grad_gate, grad_x]),
        grad_state,
        grad_step,
        grad_conv_heads,
        grad_conv_state,
        grad_bias,
        grad_decay,
        grad_skip,
        grad_inner,
        grad_out,
    )


def solution(mesh):
    in_specs = (
        P(("fsdp", "ctx"), None),
        P(("fsdp", "ctx"), None),
        P("fsdp", None),
        P("fsdp"),
        P(None, "fsdp", "tp"),
        P("fsdp", None),
        P("fsdp", "tp"),
        P("tp", None, "fsdp"),
        P(None, "fsdp"),
        P("tp"),
        P("tp"),
        P("tp"),
        P("tp", "fsdp"),
        P("tp", "fsdp"),
    )
    out_specs = (
        P(("fsdp", "ctx"), "tp"),
        P(("fsdp", "ctx"), "tp"),
        P("fsdp"),
        P(None, "fsdp", "tp"),
        P("fsdp", None),
        P("fsdp", "tp"),
        P("tp", None, "fsdp"),
        P(None, "fsdp"),
        P("tp"),
        P("tp"),
        P("tp"),
        P("tp", "fsdp"),
        P("tp", "fsdp"),
    )
    return jax.shard_map(
        per_device, mesh=mesh, in_specs=in_specs, out_specs=out_specs, check_vma=False
    )
```
